512 devices in a mesh: dp: 4 (over x_lo, core), ctx: 16 (over z), tp: 8 (over x_hi, y).
Axes of the slice: x: 4 (x_hi: 2, x_lo: 2; x = x_hi * 2 + x_lo), y: 4, z: 16, core: 2. Of those that a mesh axis runs over, the one named last changes fastest.
Arguments:
- queries: bfloat16 [4, 2048, 3072], P('dp', 'ctx', 'tp'), may hold values from -40 to 40
- key_heads: bfloat16 [4, 2048, 1024], P('dp', 'ctx', 'tp'), may hold values from -40 to 40
- value_heads: bfloat16 [4, 2048, 1024], P('dp', 'ctx', 'tp'), may hold values from -6 to 6
- doc_ids: int32 [4, 2048], P('dp', 'ctx'), may hold values from 0 to 7, never falling along the last dimension, each value on 1 to 1152 neighbouring positions
- residual: bfloat16 [4, 2048, 3072], P('dp', 'ctx', 'tp'), may hold values from -12 to 12
- ln_gain: float32 [3072], P('tp'), may hold values from 0.1 to 1.9
- expert_ids: int32 [4, 2048, 4], P('dp', 'ctx'), may hold values from 0 to 15, all different within a row; in each aligned block of 128 rows (0 to 127, 128 to 255, ..., all dimensions but the last counted through in order) at most 33 rows name the same one
- expert_weight: float32 [4, 2048, 4], P('dp', 'ctx'), may hold values from 0.3 to 1
- w_gate: bfloat16 [16, 3072, 5376], P('ctx', 'dp', 'tp'), may hold values from -0.109375 to 0.109375
- w_up: bfloat16 [16, 3072, 5376], P('ctx', 'dp', 'tp'), may hold values from -0.109375 to 0.109375
- w_down: bfloat16 [16, 5376, 3072], P('ctx', 'tp', 'dp'), may hold values from -0.078125 to 0.078125
Outputs:
- mixed: bfloat16 [4, 2048, 3072], P('dp', 'ctx', 'tp')
The draws below stay inside these ranges and needn't reach their ends.
Inputs may be any that keep to these rules, and one draw needn't show every extreme that they name: `doc_ids`: never falling along a row; each document holds at most 1152 positions and one holds exactly that many. `expert_ids`: each token names 4 different experts. Among the 128 tokens of one device no expert is named more than 33 times, a bound that some block reaches.
All inputs are finite; a program needn't handle non-finite values.
Results may differ from the reference program's by a relative error of at most 0.022.
Values may be sent and summed in bfloat16 or wider, within the bound.
No kernel may reach another device: no remote copies, remote signals or barrier semaphores. Data moves between devices by JAX's collectives and lax.ppermute only.
A program may use at most 64 MiB of HBM per device.

```python
import math
import jax
import jax.numpy as jnp
import numpy as np
from jax import lax

HEADS = 24
KV_HEADS = 8
HEAD_DIM = 128
D = 3072
FF = 5376
TOP = 4
SEQ_DEV = 128
EXPERTS = 16
LENGTH = 2048
ROWS = 4
CAP = 33
N_CTX = 16
N_TP = 8


def draw_key_heads(key, part):
    key = jax.random.fold_in(key, 5)
    result = jnp.clip(jax.random.normal(key, (ROWS, LENGTH, KV_HEADS, HEAD_DIM), jnp.float32), -6.0, 6.0)
    return result.reshape(ROWS, LENGTH, KV_HEADS * HEAD_DIM).astype(jnp.bfloat16)


def draw_queries(key, part):
    key = jax.random.fold_in(key, 6)
    group = HEADS // KV_HEADS
    result = jnp.clip(jax.random.normal(key, (ROWS, LENGTH, KV_HEADS, group, HEAD_DIM), jnp.float32), -6.0, 6.0)
    return result.reshape(ROWS, LENGTH, HEADS * HEAD_DIM).astype(jnp.bfloat16)


def draw_residual(key, part):
    key = jax.random.fold_in(key, 7)
    column = jnp.arange(D, dtype=jnp.float32)
    rough = jnp.exp(jax.random.uniform(jax.random.fold_in(key, 1), (D,), jnp.float32, 0.0, math.log(10.0)))
    col_scale = jnp.power(3.0, column / D) * rough / 30.0
    values = jnp.clip(jax.random.normal(jax.random.fold_in(key, 3), (ROWS, LENGTH, D), jnp.float32), -6.0, 6.0)
    return (values * col_scale).astype(jnp.bfloat16)


def levels(rng, extent, shards, least, high):
    level = 1.0
    for position, parts in shards:
        draws = jax.random.uniform(jax.random.fold_in(jax.random.fold_in(rng, 6), position), (parts,), jnp.float32, least / len(shards), high / len(shards))
        level = level * jnp.repeat(jnp.exp(draws), extent[position] // parts).reshape((-1,) + (1,) * (len(extent) - 1 - position))
    return level


def length_profile(amount, total, reach, lean):
    portions = [(1 << 20) // math.isqrt(standing ** lean) + 1 for standing in range(2, amount + 1)]
    spare, given = total - reach - (amount - 1), [1] * (amount - 1)
    while spare > 0:
        movable = [i for i in range(amount - 1) if given[i] < reach]
        mass, left = sum([portions[i] for i in movable]), spare
        for i in movable:
            more = min(reach - given[i], max(1, left * portions[i] // mass), spare)
            given[i] = given[i] + more
            spare = spare - more
    return np.array([reach] + given)


def ragged(key, count, total, bound, slope):
    if count == 2:
        one = jax.random.randint(key, (), max(1, total - bound), min(bound, total - 1) + 1)
        return jnp.stack([one, total - one])
    lengths = jnp.asarray(length_profile(count, total, bound, slope), jnp.int32)
    pairs = (count - 1) // 2
    giver, receiver = lengths[1:1 + 2 * pairs:2], lengths[2:2 + 2 * pairs:2]
    slack = jnp.minimum(giver - 1, bound - receiver)
    shifted = jax.random.randint(jax.random.fold_in(key, 1), (pairs,), 0, 1 << 20) % (slack + 1)
    lengths = lengths.at[1:1 + 2 * pairs:2].set(giver - shifted).at[2:2 + 2 * pairs:2].set(receiver + shifted)
    return lengths[jax.random.permutation(jax.random.fold_in(key, 2), count)]


def assign_block(stream_key, own, number, rows, number_of, top, reach, lean):
    ranking = jax.random.permutation(stream_key, number_of)
    heavy_load, common = portions_of(number_of, rows * top, reach, lean, True), portions_of(number_of, rows * top, reach, lean, False)
    places = jnp.arange(number_of)

    def named(tallies, offset_by):
        used = int((tallies > 0).sum())
        fixed = max(1, used // 4)
        passed = fixed + (places - fixed + offset_by * (used - fixed)) % max(1, number_of - fixed)
        return jnp.zeros((number_of,), jnp.int32).at[ranking[jnp.where(places < fixed, places, passed)]].set(jnp.asarray(tallies, jnp.int32))

    tallies = jnp.where(number % 4 == 0, named(heavy_load, number // 4), named(common, number - number // 4 - 1))
    mixed = jax.random.permutation(jax.random.fold_in(own, 3), number_of)
    giver, sink = mixed[0:number_of // 2 * 2:2], mixed[1:number_of // 2 * 2:2]
    slack = jnp.minimum(tallies[giver] - 1, reach - tallies[sink]) // 2
    slack = jnp.where((giver == ranking[0]) | (sink == ranking[0]) | (tallies[sink] == 0), 0, jnp.maximum(slack, 0))
    passed = jax.random.randint(jax.random.fold_in(own, 4), (number_of // 2,), 0, 1 << 20) % (slack + 1)
    tallies = tallies.at[giver].add(-passed).at[sink].add(passed)
    members = jnp.searchsorted(jnp.cumsum(tallies), jnp.arange(rows * top), side="right").astype(jnp.int32)
    listing = members.reshape(top, rows).T
    listing = listing[jax.random.permutation(jax.random.fold_in(own, 1), rows)]
    offset_by = jax.random.randint(jax.random.fold_in(own, 2), (rows, 1), 0, top)
    return jnp.take_along_axis(listing, (jnp.arange(top)[None, :] + offset_by) % top, axis=1)


def portions_of(number_of, total, bound, lean, full):
    portions = [(1 << 20) // math.isqrt(standing ** lean) + 1 for standing in range(1, number_of + 1)]
    largest = bound if full else min(bound, max(-(-total // number_of), total * portions[0] // sum(portions)))
    least = 1 if total - largest >= number_of - 1 else 0
    given, spare = [largest] + [least] * (number_of - 1), total - largest - least * (number_of - 1)
    while spare > 0:
        candidates = [i for i in range(1, number_of) if given[i] < largest] or [i for i in range(1, number_of) if given[i] < bound]
        mass, budget = sum([portions[i] for i in candidates]), spare
        for i in candidates:
            addition = min(bound - given[i], max(1, budget * portions[i] // mass), spare)
            given[i] = given[i] + addition
            spare = spare - addition
    return np.array(given)


def scatter_about(key, dims, scale, limit, pieces=(), kind=jnp.bfloat16):
    values = jax.random.normal(key, dims, jnp.float32) * scale
    if len(pieces) > 0:
        values = levels(key, dims, pieces, -0.22, 0.18) * values
    return jnp.clip(values, min=-limit, max=limit).astype(kind)


def setup_inputs(seed: int = 0) -> dict:
    seeds = jax.random.split(jax.random.key(seed), 12)
    queries = draw_queries(jax.random.fold_in(seeds[11], 71), 0)
    key_heads = draw_key_heads(jax.random.fold_in(seeds[11], 71), 0)
    value_heads = scatter_about(seeds[2], (ROWS, LENGTH, KV_HEADS * HEAD_DIM), 1.0, 6.0, ((0, 4), (1, 16), (2, 8)))
    doc_ids = jax.vmap(lambda own: jnp.searchsorted(jnp.cumsum(ragged(own, 8, LENGTH, LENGTH // 2 + SEQ_DEV, 1)), jnp.arange(LENGTH), side="right"))(jax.random.split(seeds[3], ROWS)).reshape((ROWS, LENGTH)).astype(jnp.int32)
    residual = draw_residual(jax.random.fold_in(seeds[11], 71), 0)
    ln_gain = jnp.clip(1.0 + 0.18 * jax.random.normal(seeds[5], (D,), jnp.float32), 0.1, 1.9)
    expert_ids_keys = jax.random.split(jax.random.fold_in(seeds[6], 1), ROWS * LENGTH // SEQ_DEV)
    expert_ids_turns = jax.random.permutation(jax.random.fold_in(seeds[6], 3), ROWS * LENGTH // SEQ_DEV)
    expert_ids = jax.vmap(lambda own, number: assign_block(jax.random.fold_in(seeds[6], 2), own, number, SEQ_DEV, EXPERTS, TOP, CAP, 0))(expert_ids_keys, expert_ids_turns).reshape((ROWS, LENGTH, TOP))
    expert_weight = jnp.clip(0.3 + 0.7 * jax.random.uniform(seeds[7], (ROWS, LENGTH, TOP), jnp.float32) ** levels(seeds[7], (ROWS, LENGTH, TOP), ((0, 4), (1, 16)), -0.2, 0.2), 0.3, 1.0)
    w_gate = scatter_about(seeds[8], (EXPERTS, D, FF), D ** -0.5, 0.109375, ((0, 16), (1, 4), (2, 8)))
    w_up = scatter_about(seeds[9], (EXPERTS, D, FF), D ** -0.5, 0.109375, ((0, 16), (1, 4), (2, 8)))
    w_down = scatter_about(seeds[10], (EXPERTS, FF, D), FF ** -0.5, 0.078125, ((0, 16), (1, 8), (2, 4)))
    return {"queries": queries, "key_heads": key_heads, "value_heads": value_heads, "doc_ids": doc_ids, "residual": residual, "ln_gain": ln_gain, "expert_ids": expert_ids, "expert_weight": expert_weight, "w_gate": w_gate, "w_up": w_up, "w_down": w_down}


def slot_table(route_block, expert_count, capacity):
    flat_ids = route_block.reshape(-1).astype(jnp.int32)
    onehot = (flat_ids[:, None] == jnp.arange(expert_count, dtype=jnp.int32)[None, :]).astype(jnp.int32)
    ranks = jnp.cumsum(onehot, axis=0) - 1
    placed = lax.optimization_barrier(jnp.sum(onehot * ranks, axis=1)).astype(jnp.int32)
    slot_of = (flat_ids * capacity + placed).astype(jnp.int32)
    token_ids = (jnp.arange(flat_ids.shape[0], dtype=jnp.int32) // route_block.shape[1]).astype(jnp.int32)
    token_of = jnp.zeros((expert_count * capacity,), jnp.int32).at[slot_of].set(token_ids)
    filled = jnp.zeros((expert_count * capacity,), jnp.bfloat16).at[slot_of].set(jnp.ones_like(slot_of, dtype=jnp.bfloat16))
    return (slot_of.reshape(route_block.shape), token_of, filled)

def reference(queries, key_heads, value_heads, doc_ids, residual, ln_gain, expert_ids, expert_weight, w_gate, w_up, w_down):
    group = HEADS // KV_HEADS
    block_len = min(512, LENGTH)
    scale = 1.0 / math.sqrt(HEAD_DIM)
    place = jnp.arange(LENGTH, dtype=jnp.int32)

    def attend_row(row_args):
        query_row, key_row, value_row, docs = row_args
        query_split = query_row.reshape(LENGTH, KV_HEADS, group, HEAD_DIM).transpose(1, 0, 2, 3)
        key_split = key_row.reshape(LENGTH, KV_HEADS, HEAD_DIM).transpose(1, 0, 2)
        value_split = value_row.reshape(LENGTH, KV_HEADS, HEAD_DIM).transpose(1, 0, 2)

        def attend_head(head_args):
            query_head, key_head, value_head = head_args
            query_blocks = query_head.reshape(LENGTH // block_len, block_len, group, HEAD_DIM)
            firsts = jnp.arange(LENGTH // block_len, dtype=jnp.int32) * block_len

            def one_block(block_args):
                query_part, first = block_args
                scores = jnp.einsum('tgd,nd->tgn', query_part.astype(jnp.float32), key_head.astype(jnp.float32)) * scale
                rows_place = first + jnp.arange(block_len, dtype=jnp.int32)
                row_docs = lax.dynamic_slice_in_dim(docs, first, block_len)
                allowed = (place[None, :] <= rows_place[:, None]) & (docs[None, :] == row_docs[:, None])
                allowed = allowed[:, None, :]
                masked = jnp.where(allowed, scores, jnp.float32(-1e+30))
                highest = lax.optimization_barrier(jnp.max(masked, axis=-1, keepdims=True))
                weights = jnp.where(allowed, jnp.exp(masked - highest), jnp.float32(0.0))
                total = lax.optimization_barrier(jnp.sum(weights, axis=-1))
                rounded = weights.astype(jnp.bfloat16)
                summed = jnp.einsum('tgn,nd->tgd', rounded.astype(jnp.float32), value_head.astype(jnp.float32))
                return summed / total[..., None]
            return lax.map(one_block, (query_blocks, firsts)).reshape(LENGTH, group, HEAD_DIM)
        heads_out = lax.map(attend_head, (query_split, key_split, value_split))
        return heads_out.transpose(1, 0, 2, 3).reshape(LENGTH, D).astype(jnp.bfloat16)
    attn = lax.map(attend_row, (queries, key_heads, value_heads, doc_ids))
    post = residual.astype(jnp.float32) + attn.astype(jnp.float32)
    average = lax.optimization_barrier(jnp.mean(post, axis=-1, keepdims=True))
    spread = lax.optimization_barrier(jnp.mean(post * post, axis=-1, keepdims=True)) - average * average
    normed = ((post - average) * lax.rsqrt(spread + 1e-05) * ln_gain.astype(jnp.float32)).astype(jnp.bfloat16)
    blocks = ROWS * N_CTX
    normed_blocks = normed.reshape(blocks, SEQ_DEV, D)
    route_blocks = expert_ids.reshape(blocks, SEQ_DEV, TOP)
    weight_blocks = expert_weight.reshape(blocks, SEQ_DEV, TOP)
    slot_of, token_of, filled = jax.vmap(lambda rb: slot_table(rb, EXPERTS, CAP))(route_blocks)
    sent = jax.vmap(lambda nb, tb, fb: nb[tb] * fb[:, None])(normed_blocks, token_of, filled)
    sent = sent.reshape(blocks, EXPERTS, CAP, D).transpose(1, 0, 2, 3).reshape(EXPERTS, blocks * CAP, D)
    group_ff = FF // N_TP

    def run_expert(expert_args):
        rows_in, gate_mat, up_mat, down_mat = expert_args
        gate = jnp.dot(rows_in, gate_mat, preferred_element_type=jnp.float32)
        up_val = jnp.dot(rows_in, up_mat, preferred_element_type=jnp.float32)
        hidden = (jax.nn.silu(gate) * up_val).astype(jnp.bfloat16)
        total = jnp.zeros((rows_in.shape[0], D), jnp.float32)
        for part_idx in range(N_TP):
            lower = part_idx * group_ff
            partial_val = jnp.dot(hidden[:, lower:lower + group_ff], down_mat[lower:lower + group_ff, :], preferred_element_type=jnp.float32)
            partial_val = lax.optimization_barrier(partial_val.astype(jnp.bfloat16))
            total = total + partial_val.astype(jnp.float32)
        return total.astype(jnp.bfloat16)
    outputs = lax.map(run_expert, (sent, w_gate, w_up, w_down))
    outputs = outputs.reshape(EXPERTS, blocks, CAP, D).transpose(1, 0, 2, 3).reshape(blocks, EXPERTS * CAP, D)

    def combine(comb_args):
        block_out, block_slots, block_weight = comb_args
        picked = block_out[block_slots].astype(jnp.float32)
        return lax.optimization_barrier(jnp.sum(block_weight[..., None] * picked, axis=1))
    moe_out = lax.map(combine, (outputs, slot_of, weight_blocks)).reshape(ROWS, LENGTH, D)
    return (post + moe_out).astype(jnp.bfloat16)
```

```python
import functools
import math

import jax
import jax.numpy as jnp
from jax import lax
from jax.experimental import pallas as pl
from jax.experimental.pallas import tpu as pltpu
from jax.sharding import PartitionSpec as P

HEAD_DIM = 128
CAP = 33
REACH = 1152
BF = jnp.bfloat16
F32 = jnp.float32
VMEM = pl.BlockSpec(memory_space=pltpu.VMEM)
SMEM = pl.BlockSpec(memory_space=pltpu.SMEM)
ANY = pl.BlockSpec(memory_space=pl.ANY)
NN = (((1,), (0,)), ((), ()))
NT = (((1,), (1,)), ((), ()))
TN = (((0,), (0,)), ((), ()))


def dot(a, b, dims=NN):
    return lax.dot_general(a, b, dims, preferred_element_type=F32)


def call(body, out, specs, scratch=(), limit=32 << 20, flops=0, moved=0, name=None):
    return pl.pallas_call(
        body,
        out_shape=out,
        in_specs=specs,
        out_specs=jax.tree.map(lambda _: VMEM, out),
        scratch_shapes=list(scratch),
        compiler_params=pltpu.CompilerParams(vmem_limit_bytes=limit),
        cost_estimate=pl.CostEstimate(flops=flops, bytes_accessed=moved, transcendentals=0),
        name=name,
    )


def attend_kernel(back, v_first, place_ref, q_ref, kv_ref, rest_ref, docs_ref, res_ref, post_ref, stat_ref, scores):
    here = place_ref[0]
    rows, wide = q_ref.shape
    group = wide // HEAD_DIM
    scale = 1.0 / math.sqrt(HEAD_DIM)
    q = jnp.concatenate([q_ref[:, g * HEAD_DIM : (g + 1) * HEAD_DIM] for g in range(group)], axis=0)
    own = jnp.concatenate([docs_ref[...]] * group, axis=0)
    low = jnp.maximum(here - back, 0)
    row = lax.rem(lax.broadcasted_iota(jnp.int32, (group * rows, rows), 0), rows)
    col = lax.broadcasted_iota(jnp.int32, (group * rows, rows), 1)
    ahead = col - row
    docs_at = rows + v_first

    def first(j, top):
        s = dot(q, kv_ref[j, 0:rows, :], NT) * scale
        docs = kv_ref[j, docs_at : docs_at + 8, :][0:1, :].astype(F32)
        allowed = (docs == own) & (ahead <= (here - j) * rows)
        s = jnp.where(allowed, s, -1e30)
        scores[j - low] = s
        return jnp.maximum(top, s)

    top = lax.fori_loop(low, here + 1, first, jnp.full((group * rows, rows), -1e30, F32))
    top = jnp.max(top, axis=1, keepdims=True)

    def second(j, carry):
        total, added = carry
        s = scores[j - low]
        w = jnp.where(s > -1e29, jnp.exp(s - top), 0.0)
        values = jnp.concatenate([kv_ref[j, rows : rows + v_first, :], rest_ref[j]], axis=0)
        return total + w, added + dot(w.astype(BF), values)

    zero = jnp.zeros((group * rows, rows), F32)
    total, added = lax.fori_loop(low, here + 1, second, (zero, jnp.zeros((group * rows, HEAD_DIM), F32)))
    attn = (added / jnp.sum(total, axis=1, keepdims=True)).astype(BF).astype(F32)
    attn = jnp.concatenate([attn[g * rows : (g + 1) * rows] for g in range(group)], axis=1)
    post = res_ref[...].astype(F32) + attn
    post_ref[...] = post
    ones = jnp.ones((rows, rows), F32)
    stat_ref[0:1, :] = (jnp.sum(post, axis=1, keepdims=True) * ones).T[0:1]
    stat_ref[1:2, :] = (jnp.sum(post * post, axis=1, keepdims=True) * ones).T[0:1]
    stat_ref[2:8, :] = jnp.zeros((6, rows), F32)


def named_and_rank(ids_ref, experts):
    tokens = ids_ref.shape[1]
    expert = lax.broadcasted_iota(jnp.int32, (experts, tokens), 0)
    named = jnp.zeros((experts, tokens), F32)
    for k in range(ids_ref.shape[0]):
        named = named + jnp.where(ids_ref[k : k + 1, :] == expert, 1.0, 0.0)
    before = lax.broadcasted_iota(jnp.int32, (tokens, tokens), 0) < lax.broadcasted_iota(jnp.int32, (tokens, tokens), 1)
    rank = dot(named.astype(BF), jnp.where(before, 1.0, 0.0).astype(BF))
    return jnp.where(named > 0.5, rank, -10000.0)


def dispatch_kernel(width, post_ref, stat_ref, gain_ref, ids_ref, out_ref):
    post = post_ref[...]
    tokens, features = post.shape
    experts, rows, lanes = out_ref.shape
    stat = jnp.sum(stat_ref[...], axis=0)
    ones = jnp.ones((tokens, tokens), F32)
    average = (stat[0:1, :] * ones).T[:, 0:1] / width
    spread = (stat[1:2, :] * ones).T[:, 0:1] / width - average * average
    normed = ((post - average) * lax.rsqrt(spread + 1e-5) * gain_ref[...]).astype(BF)
    groups = features // lanes
    stacked = jnp.concatenate([normed[:, g * lanes : (g + 1) * lanes] for g in range(groups)], axis=0)
    rank = named_and_rank(ids_ref, experts).astype(jnp.int32)
    wanted = jnp.concatenate([rank + g * CAP for g in range(groups)], axis=1)
    row = lax.broadcasted_iota(jnp.int32, (rows, groups * tokens), 0)
    for e in range(experts):
        pick = jnp.where(row == wanted[e : e + 1, :], 1.0, 0.0).astype(BF)
        out_ref[e] = dot(pick, stacked).astype(BF)


def spread_kernel(in_ref, out_ref, flat):
    blocks, _, lanes = in_ref.shape
    copies, _, features = out_ref.shape
    for b in range(blocks):
        block = in_ref[b].astype(F32)
        for g in range(features // lanes):
            flat[b * CAP : (b + 1) * CAP, g * lanes : (g + 1) * lanes] = block[g * CAP : (g + 1) * CAP]
    rows = flat[...].astype(BF)
    for c in range(copies):
        out_ref[c] = rows


def expert_kernel(dp_ref, x_ref, w0, w1, w2, w3, out_ref, held, gate, up, hidden, sems):
    dp = dp_ref[0]
    order = [(p, m) for p in range(4) for m in (0, 1)] + [(p, 2) for p in range(4)]
    copies = {}
    for p, m in order:
        source = (w0, w1, w2, w3)[p]
        copies[p, m] = pltpu.make_async_copy(source.at[m], held.at[p, m], sems.at[p, m])
        copies[p, m].start()
    for p in range(4):
        j = dp ^ p
        copies[p, 0].wait()
        copies[p, 1].wait()
        x = jnp.concatenate([x_ref[2 * j], x_ref[2 * j + 1]], axis=1)
        g = dot(x, held[p, 0], NT)
        u = dot(x, held[p, 1], NT)
        if p == 0:
            gate[...] = g
            up[...] = u
        elif p < 3:
            gate[...] += g
            up[...] += u
        else:
            g = gate[...] + g
            u = up[...] + u
            hidden[...] = (g / (1.0 + jnp.exp(-g)) * u).astype(BF)
    for p in range(4):
        j = dp ^ p
        copies[p, 2].wait()
        y = dot(hidden[...], held[p, 2]).astype(BF)
        half = y.shape[1] // 2
        out_ref[2 * j] = y[:, :half]
        out_ref[2 * j + 1] = y[:, half:]


def total_kernel(in_ref, out_ref, flat):
    parts, _, features = in_ref.shape
    blocks, rows, lanes = out_ref.shape
    total = in_ref[0].astype(F32)
    for p in range(1, parts):
        total = total + in_ref[p].astype(F32)
    flat[...] = total
    groups = features // lanes
    for b in range(blocks):
        block = flat[b * CAP : (b + 1) * CAP, :]
        runs = [block[:, g * lanes : (g + 1) * lanes] for g in range(groups)]
        runs.append(jnp.zeros((rows - groups * CAP, lanes), F32))
        out_ref[b] = jnp.concatenate(runs, axis=0).astype(BF)


def combine_kernel(post_ref, ids_ref, weight_ref, back_ref, out_ref):
    tokens, features = post_ref.shape
    experts, rows, lanes = back_ref.shape
    groups = features // lanes
    rank = named_and_rank(ids_ref, experts).astype(jnp.int32)
    expert = lax.broadcasted_iota(jnp.int32, (experts, tokens), 0)
    weight = jnp.zeros((experts, tokens), F32)
    for k in range(ids_ref.shape[0]):
        weight = weight + jnp.where(ids_ref[k : k + 1, :] == expert, weight_ref[k : k + 1, :], 0.0)
    wide_rank = jnp.concatenate([rank + g * CAP for g in range(groups)], axis=1)
    wide_weight = jnp.concatenate([weight] * groups, axis=1)
    row = lax.broadcasted_iota(jnp.int32, (rows, groups * tokens), 0)
    moe = jnp.zeros((groups * tokens, lanes), F32)
    for e in range(experts):
        pick = jnp.where(row == wide_rank[e : e + 1, :], wide_weight[e : e + 1, :], 0.0)
        upper = pick.astype(BF)
        lower = (pick - upper.astype(F32)).astype(BF)
        moe = moe + dot(upper, back_ref[e], TN) + dot(lower, back_ref[e], TN)
    moe = jnp.concatenate([moe[g * tokens : (g + 1) * tokens] for g in range(groups)], axis=1)
    out_ref[...] = (post_ref[...] + moe).astype(BF)


def all_to_all(x, axis):
    return lax.all_to_all(x, axis, split_axis=0, concat_axis=0, tiled=True)


def on_device(
    queries,
    key_heads,
    value_heads,
    doc_ids,
    residual,
    ln_gain,
    expert_ids,
    expert_weight,
    w_gate,
    w_up,
    w_down,
):
    rows = queries.shape[1]
    features = residual.shape[2]
    ctx_count = lax.axis_size("ctx")
    tp_count = lax.axis_size("tp")
    dp_index = lax.axis_index("dp").reshape(1)
    ctx_index = lax.axis_index("ctx").reshape(1)
    ids = expert_ids[0].T
    weight = expert_weight[0].T
    hidden_units = w_down.shape[1]

    w_own = jnp.stack([w_gate[0].T, w_up[0].T, w_down[0]])
    other_chip = [(i, i ^ 2) for i in range(4)]
    other_core = [(i, i ^ 1) for i in range(4)]
    w_chip = lax.ppermute(w_own, "dp", other_chip)
    w_core = lax.ppermute(w_own, "dp", other_core)

    v_first = rows - 16
    docs_row = jnp.broadcast_to(doc_ids.astype(BF), (8, rows))
    packed = jnp.concatenate([key_heads[0], value_heads[0, :v_first], docs_row], axis=0)
    rest = all_to_all(jnp.broadcast_to(value_heads[:, v_first:], (ctx_count, rows - v_first, HEAD_DIM)), "ctx")
    kv = lax.all_gather(packed, "ctx", axis=0)
    back = -(-(REACH - 1) // rows)
    group = queries.shape[2] // HEAD_DIM
    post, stat = call(
        functools.partial(attend_kernel, back, v_first),
        (jax.ShapeDtypeStruct((rows, features), F32), jax.ShapeDtypeStruct((8, rows), F32)),
        [SMEM] + [VMEM] * 5,
        [pltpu.VMEM((back + 1, group * rows, rows), F32)],
        name="attend",
    )(ctx_index, queries[0], kv, rest, doc_ids[0].astype(F32).reshape(rows, 1), residual[0])

    stats = all_to_all(jnp.broadcast_to(stat[None], (tp_count,) + stat.shape), "tp")
    block = -(-(features // 128 * CAP) // 8) * 8
    outgoing = call(
        functools.partial(dispatch_kernel, features * tp_count),
        jax.ShapeDtypeStruct((ctx_count, block, 128), BF),
        [VMEM] * 4,
        name="dispatch",
    )(post, stats, ln_gain.reshape(1, features), ids)
    landed = all_to_all(outgoing, "ctx")
    landed, w_chip = lax.optimization_barrier((landed, w_chip))
    w_both = lax.ppermute(w_chip, "dp", other_core)
    total_rows = ctx_count * CAP
    copies = call(
        spread_kernel,
        jax.ShapeDtypeStruct((tp_count, total_rows, features), BF),
        [VMEM],
        [pltpu.VMEM((total_rows, features), F32)],
        name="spread",
    )(landed)
    arrived = all_to_all(copies, "tp")
    partial = call(
        expert_kernel,
        jax.ShapeDtypeStruct((tp_count, total_rows, features), BF),
        [SMEM, VMEM, ANY, ANY, ANY, ANY],
        [
            pltpu.VMEM((4, 3, hidden_units, w_down.shape[2]), BF),
            pltpu.VMEM((total_rows, hidden_units), F32),
            pltpu.VMEM((total_rows, hidden_units), F32),
            pltpu.VMEM((total_rows, hidden_units), BF),
            pltpu.SemaphoreType.DMA((4, 3)),
        ],
        limit=48 << 20,
        flops=6 * total_rows * hidden_units * features * tp_count,
        moved=24 << 20,
        name="expert",
    )(dp_index, arrived, w_own, w_core, w_chip, w_both)
    groups = all_to_all(partial, "tp")
    expert_out = call(
        total_kernel,
        jax.ShapeDtypeStruct((ctx_count, block, 128), BF),
        [VMEM],
        [pltpu.VMEM((total_rows, features), F32)],
        name="total",
    )(groups)
    returned = all_to_all(expert_out, "ctx")
    mixed = call(
        combine_kernel,
        jax.ShapeDtypeStruct((rows, features), BF),
        [VMEM] * 4,
        name="combine",
    )(post, ids, weight, returned)
    return mixed[None]


def solution(mesh):
    placed = (
        P("dp", "ctx", "tp"),
        P("dp", "ctx", "tp"),
        P("dp", "ctx", "tp"),
        P("dp", "ctx"),
        P("dp", "ctx", "tp"),
        P("tp"),
        P("dp", "ctx", None),
        P("dp", "ctx", None),
        P("ctx", "dp", "tp"),
        P("ctx", "dp", "tp"),
        P("ctx", "tp", "dp"),
    )
    return jax.shard_map(
        on_device, mesh=mesh, in_specs=placed, out_specs=P("dp", "ctx", "tp"), check_vma=False
    )
```

```python
import functools
import math

import jax
import jax.numpy as jnp
from jax import lax
from jax.experimental import pallas as pl
from jax.experimental.pallas import tpu as pltpu
from jax.sharding import PartitionSpec as P

HEAD_DIM = 128
CAP = 33
FULL = 58 << 20
REACH = 1152
BF = jnp.bfloat16
F32 = jnp.float32
VMEM = pl.BlockSpec(memory_space=pltpu.VMEM)
SMEM = pl.BlockSpec(memory_space=pltpu.SMEM)
ANY = pl.BlockSpec(memory_space=pl.ANY)
NN = (((1,), (0,)), ((), ()))
NT = (((1,), (1,)), ((), ()))
TN = (((0,), (0,)), ((), ()))


def dot(a, b, dims=NN):
    return lax.dot_general(a, b, dims, preferred_element_type=F32)


def call(body, out, specs, scratch=(), out_spec=VMEM, limit=32 << 20, flops=0, moved=0, name=None):
    return pl.pallas_call(
        body,
        out_shape=out,
        in_specs=specs,
        out_specs=jax.tree.map(lambda _: out_spec, out),
        scratch_shapes=list(scratch),
        compiler_params=pltpu.CompilerParams(vmem_limit_bytes=limit),
        cost_estimate=pl.CostEstimate(flops=flops, bytes_accessed=moved, transcendentals=0),
        name=name,
    )


def terms(x, count):
    out = []
    for _ in range(count):
        part = x.astype(BF).astype(F32)
        out.append(part)
        x = x - part
    return out


def stack_kernel(*refs):
    *sources, out_ref, held, arrive, leave = refs
    into = [pltpu.make_async_copy(source, held.at[i], arrive.at[i]) for i, source in enumerate(sources)]
    away = [pltpu.make_async_copy(held.at[i], out_ref.at[i], leave.at[i]) for i in range(len(sources))]
    for copy in into:
        copy.start()
    for first, then in zip(into, away):
        first.wait()
        then.start()
    for copy in away:
        copy.wait()


def named_and_rank(ids_ref, experts):
    tokens = ids_ref.shape[1]
    expert = lax.broadcasted_iota(jnp.int32, (experts, tokens), 0)
    named = jnp.zeros((experts, tokens), F32)
    for k in range(ids_ref.shape[0]):
        named = named + jnp.where(ids_ref[k : k + 1, :] == expert, 1.0, 0.0)
    before = lax.broadcasted_iota(jnp.int32, (tokens, tokens), 0) < lax.broadcasted_iota(jnp.int32, (tokens, tokens), 1)
    rank = dot(named.astype(BF), jnp.where(before, 1.0, 0.0).astype(BF))
    return jnp.where(named > 0.5, rank, -10000.0)


def attend_kernel(
    back, v_first, place_ref, q_ref, kv_ref, rest_ref, docs_ref, res_ref, ids_ref, post_ref, out_ref, scores
):
    here = place_ref[0]
    rows, wide = q_ref.shape
    group = wide // HEAD_DIM
    scale = 1.0 / math.sqrt(HEAD_DIM)
    q = jnp.concatenate([q_ref[:, g * HEAD_DIM : (g + 1) * HEAD_DIM] for g in range(group)], axis=0)
    own = jnp.concatenate([docs_ref[...]] * group, axis=0)
    low = jnp.maximum(here - back, 0)
    row = lax.rem(lax.broadcasted_iota(jnp.int32, (group * rows, rows), 0), rows)
    col = lax.broadcasted_iota(jnp.int32, (group * rows, rows), 1)
    ahead = col - row
    docs_at = rows + v_first

    def first(j, top):
        s = dot(q, kv_ref[j, 0:rows, :], NT) * scale
        docs = kv_ref[j, docs_at : docs_at + 8, :][0:1, :].astype(F32)
        allowed = (docs == own) & (ahead <= (here - j) * rows)
        s = jnp.where(allowed, s, -1e30)
        scores[j - low] = s
        return jnp.maximum(top, s)

    top = lax.fori_loop(low, here + 1, first, jnp.full((group * rows, rows), -1e30, F32))
    top = jnp.max(top, axis=1, keepdims=True)

    def second(j, carry):
        total, added = carry
        s = scores[j - low]
        w = jnp.where(s > -1e29, jnp.exp(s - top), 0.0)
        values = jnp.concatenate([kv_ref[j, rows : rows + v_first, :], rest_ref[j]], axis=0)
        return total + w, added + dot(w.astype(BF), values)

    zero = jnp.zeros((group * rows, rows), F32)
    total, added = lax.fori_loop(low, here + 1, second, (zero, jnp.zeros((group * rows, HEAD_DIM), F32)))
    attn = (added / jnp.sum(total, axis=1, keepdims=True)).astype(BF).astype(F32)
    attn = jnp.concatenate([attn[g * rows : (g + 1) * rows] for g in range(group)], axis=1)
    post = res_ref[...].astype(F32) + attn
    post_ref[...] = post

    experts, block, lanes = out_ref.shape
    groups = wide // lanes
    mean = jnp.mean(post, axis=1, keepdims=True)
    centred = post - mean
    square = jnp.sum(centred * centred, axis=1, keepdims=True)
    centred = centred.astype(BF)
    ones = jnp.ones((rows, rows), F32)
    parts = terms((mean * ones).T[0:1], 3) + terms((square * ones).T[0:1], 2)
    parts = jnp.concatenate(parts + [jnp.zeros((3, rows), F32)], axis=0).astype(BF)
    stacked = jnp.concatenate([centred[:, g * lanes : (g + 1) * lanes] for g in range(groups)], axis=0)
    rank = named_and_rank(ids_ref, experts).astype(jnp.int32)
    wanted = jnp.concatenate([rank + g * CAP for g in range(groups)], axis=1)
    place = lax.broadcasted_iota(jnp.int32, (block, groups * rows), 0)
    slot = lax.broadcasted_iota(jnp.int32, (lanes, rows), 0)
    for e in range(experts):
        pick = jnp.where(place == wanted[e : e + 1, :], 1.0, 0.0).astype(BF)
        data = dot(pick, stacked)
        pick = jnp.where(slot == rank[e : e + 1, :], 1.0, 0.0).astype(BF)
        stats = dot(parts, pick, NT)
        out_ref[e] = jnp.concatenate([data[: groups * CAP], stats[: block - groups * CAP]], axis=0).astype(BF)


def spread_kernel(in_ref, gain_ref, out_ref, flat):
    blocks, block, lanes = in_ref.shape
    copies, _, features = out_ref.shape
    groups = features // lanes
    half = blocks // 2
    stats = []
    for b in range(blocks):
        x = in_ref[b].astype(F32)
        for g in range(groups):
            flat[b * CAP : (b + 1) * CAP, g * lanes : (g + 1) * lanes] = x[g * CAP : (g + 1) * CAP]
        stats.append(jnp.concatenate([x[groups * CAP :], jnp.zeros((8 - block + groups * CAP, lanes), F32)], axis=0))
    at = lax.broadcasted_iota(jnp.int32, (half * lanes, features), 0)
    lane = lax.broadcasted_iota(jnp.int32, (half * lanes, features), 1)
    slot = lax.rem(at, lanes)
    put = jnp.where((lane == lax.div(at, lanes) * CAP + slot) & (slot < CAP), 1.0, 0.0).astype(BF)
    top = blocks * CAP
    for h in range(2):
        mine = jnp.concatenate(stats[h * half : (h + 1) * half], axis=1).astype(BF)
        flat[top + 5 * h : top + 5 * h + 5, :] = dot(mine, put)[0:5]
    flat[top + 10 : top + 16, :] = jnp.concatenate(
        terms(gain_ref[...], 3) + [jnp.zeros((3, features), F32)], axis=0
    )
    result = flat[...].astype(BF)
    for c in range(copies):
        out_ref[c] = result


def expert_kernel(
    dp_ref, x_ref, g0, g1, g2, g3, d0, d1, d2, d3, out_ref, x_in, tails, held, gate, up, hidden, column, y_out, sems, more
):
    dp = dp_ref[0]
    parts, total, features = x_ref.shape
    rows = total - 16
    half = rows // 2
    arriving = {("tails",): pltpu.make_async_copy(x_ref.at[:, pl.ds(rows, 16), :], tails, more.at[8])}
    for p in range(4):
        for i in range(2):
            source = x_ref.at[2 * (dp ^ p) + i, pl.ds(0, rows), :]
            arriving["x", p, i] = pltpu.make_async_copy(source, x_in.at[2 * p + i], more.at[2 * p + i])
        for m in range(3):
            source = (d0, d1, d2, d3)[p] if m == 2 else (g0, g1, g2, g3)[p].at[m]
            arriving[p, m] = pltpu.make_async_copy(source, held.at[p, m], sems.at[p, m])

    def begin(*keys):
        for key in keys:
            arriving[key].start()

    def piece(p):
        return ("x", p, 0), ("x", p, 1), (p, 0), (p, 1)

    begin(("tails",), *piece(0))
    arriving["tails",].wait()
    begin(*piece(1))
    means, squares = [], []
    for q in range(parts):
        tail = tails[q].astype(F32)
        means.append([tail[5 * h : 5 * h + 1] + tail[5 * h + 1 : 5 * h + 2] + tail[5 * h + 2 : 5 * h + 3] for h in (0, 1)])
        squares.append([tail[5 * h + 3 : 5 * h + 4] + tail[5 * h + 4 : 5 * h + 5] for h in (0, 1)])
    for h in (0, 1):
        average = sum(m[h] for m in means) / parts
        shifts = [m[h] - average for m in means]
        spread = (sum(s[h] for s in squares) + features * sum(s * s for s in shifts)) / (parts * features)
        block = jnp.concatenate(shifts + [lax.rsqrt(spread + 1e-5), jnp.zeros((128 - parts - 1, features), F32)], axis=0)
        column[h * half : (h + 1) * half, :] = block.T[0:half]

    def normed(p, i):
        q = 2 * (dp ^ p) + i
        tail = tails[q].astype(F32)
        gain = tail[10:11] + tail[11:12] + tail[12:13]
        at = lax.broadcasted_iota(jnp.int32, (rows, 128), 1)
        shift = jnp.sum(jnp.where(at == q, column[...], 0.0), axis=1, keepdims=True)
        scale = column[:, parts : parts + 1]
        arriving["x", p, i].wait()
        return ((x_in[2 * p + i].astype(F32) + shift) * scale * gain).astype(BF)

    for p in range(4):
        x = jnp.concatenate([normed(p, 0), normed(p, 1)], axis=1)
        arriving[p, 0].wait()
        arriving[p, 1].wait()
        if p < 2:
            begin(*piece(p + 2))
        else:
            begin((2 * p - 4, 2), (2 * p - 3, 2))
        g = dot(x, held[p, 0], NT)
        u = dot(x, held[p, 1], NT)
        if p == 0:
            gate[...] = g
            up[...] = u
        elif p < 3:
            gate[...] += g
            up[...] += u
        else:
            g = gate[...] + g
            u = up[...] + u
            hidden[...] = (g / (1.0 + jnp.exp(-g)) * u).astype(BF)
    leaving = []
    for p in range(4):
        j = dp ^ p
        arriving[p, 2].wait()
        y = dot(hidden[...], held[p, 2]).astype(BF)
        for i in range(2):
            y_out[2 * p + i] = y[:, i * features : (i + 1) * features]
            leaving.append(pltpu.make_async_copy(y_out.at[2 * p + i], out_ref.at[2 * j + i], more.at[9 + 2 * p + i]))
            leaving[-1].start()
    for copy in leaving:
        copy.wait()


def total_kernel(in_ref, out_ref, flat):
    parts, _, features = in_ref.shape
    blocks, rows, lanes = out_ref.shape
    total = in_ref[0].astype(F32)
    for p in range(1, parts):
        total = total + in_ref[p].astype(F32)
    flat[...] = total
    groups = features // lanes
    for b in range(blocks):
        block = flat[b * CAP : (b + 1) * CAP, :]
        runs = [block[:, g * lanes : (g + 1) * lanes] for g in range(groups)]
        runs.append(jnp.zeros((rows - groups * CAP, lanes), F32))
        out_ref[b] = jnp.concatenate(runs, axis=0).astype(BF)


def weigh_kernel(term, ids_ref, weight_ref, out_ref):
    experts, rows, wide = out_ref.shape
    tokens = ids_ref.shape[1]
    groups = wide // tokens
    rank = named_and_rank(ids_ref, experts).astype(jnp.int32)
    expert = lax.broadcasted_iota(jnp.int32, (experts, tokens), 0)
    weight = jnp.zeros((experts, tokens), F32)
    for k in range(ids_ref.shape[0]):
        weight = weight + jnp.where(ids_ref[k : k + 1, :] == expert, weight_ref[k : k + 1, :], 0.0)
    weight = terms(weight, 2)[term]
    wide_rank = jnp.concatenate([rank + g * CAP for g in range(groups)], axis=1)
    wide_weight = jnp.concatenate([weight] * groups, axis=1)
    row = lax.broadcasted_iota(jnp.int32, (rows, wide), 0)
    for e in range(experts):
        out_ref[e] = jnp.where(row == wide_rank[e : e + 1, :], wide_weight[e : e + 1, :], 0.0).astype(BF)


def combine_kernel(post_ref, upper_ref, lower_ref, back_ref, out_ref):
    tokens, features = post_ref.shape
    experts, rows, lanes = back_ref.shape
    groups = features // lanes
    moe = jnp.zeros((groups * tokens, lanes), F32)
    for e in range(experts):
        moe = moe + dot(upper_ref[e], back_ref[e], TN) + dot(lower_ref[e], back_ref[e], TN)
    moe = jnp.concatenate([moe[g * tokens : (g + 1) * tokens] for g in range(groups)], axis=1)
    out_ref[...] = (post_ref[...] + moe).astype(BF)


def all_to_all(x, axis):
    return lax.all_to_all(x, axis, split_axis=0, concat_axis=0, tiled=True)


def on_device(
    queries,
    key_heads,
    value_heads,
    doc_ids,
    residual,
    ln_gain,
    expert_ids,
    expert_weight,
    w_gate,
    w_up,
    w_down,
):
    rows = queries.shape[1]
    features = residual.shape[2]
    ctx_count = lax.axis_size("ctx")
    tp_count = lax.axis_size("tp")
    dp_index = lax.axis_index("dp").reshape(1)
    ctx_index = lax.axis_index("ctx").reshape(1)
    ids = expert_ids[0].T
    weight = expert_weight[0].T
    hidden_units = w_down.shape[1]

    other_chip = [(i, i ^ 2) for i in range(4)]
    other_core = [(i, i ^ 1) for i in range(4)]
    down = w_down[0]
    both = call(
        stack_kernel,
        jax.ShapeDtypeStruct((2,) + down.shape, BF),
        [ANY, ANY],
        [pltpu.VMEM((2,) + down.shape, BF), pltpu.SemaphoreType.DMA((2,)), pltpu.SemaphoreType.DMA((2,))],
        out_spec=ANY,
        limit=FULL,
        name="stack",
    )(w_gate[0].T, w_up[0].T)
    both_chip = lax.ppermute(both, "dp", other_chip)

    v_first = rows - 16
    docs_row = jnp.broadcast_to(doc_ids.astype(BF), (8, rows))
    packed = jnp.concatenate([key_heads[0], value_heads[0, :v_first], docs_row], axis=0)
    rest = all_to_all(jnp.broadcast_to(value_heads[:, v_first:], (ctx_count, rows - v_first, HEAD_DIM)), "ctx")
    kv = lax.all_gather(packed, "ctx", axis=0)
    back = -(-(REACH - 1) // rows)
    group = queries.shape[2] // HEAD_DIM
    block = -(-(features // 128 * CAP + 5) // 8) * 8
    post, outgoing = call(
        functools.partial(attend_kernel, back, v_first),
        (jax.ShapeDtypeStruct((rows, features), F32), jax.ShapeDtypeStruct((ctx_count, block, 128), BF)),
        [SMEM] + [VMEM] * 6,
        [pltpu.VMEM((back + 1, group * rows, rows), F32)],
        name="attend",
    )(ctx_index, queries[0], kv, rest, doc_ids[0].astype(F32).reshape(rows, 1), residual[0], ids)
    outgoing, down, both, both_chip = lax.optimization_barrier((outgoing, down, both, both_chip))
    landed = all_to_all(outgoing, "ctx")
    down_chip = lax.ppermute(down, "dp", other_chip)
    both_core = lax.ppermute(both, "dp", other_core)
    both_far = lax.ppermute(both_chip, "dp", other_core)
    down_core = lax.ppermute(down, "dp", other_core)
    total_rows = ctx_count * CAP
    copies = call(
        spread_kernel,
        jax.ShapeDtypeStruct((tp_count, total_rows + 16, features), BF),
        [VMEM] * 2,
        [pltpu.VMEM((total_rows + 16, features), F32)],
        name="spread",
    )(landed, ln_gain.reshape(1, features))
    copies, down_chip = lax.optimization_barrier((copies, down_chip))
    arrived = all_to_all(copies, "tp")
    down_far = lax.ppermute(down_chip, "dp", other_core)
    partial = call(
        expert_kernel,
        jax.ShapeDtypeStruct((tp_count, total_rows, features), BF),
        [SMEM] + [ANY] * 9,
        [
            pltpu.VMEM((tp_count, total_rows, features), BF),
            pltpu.VMEM((tp_count, 16, features), BF),
            pltpu.VMEM((4, 3) + down.shape, BF),
            pltpu.VMEM((total_rows, hidden_units), F32),
            pltpu.VMEM((total_rows, hidden_units), F32),
            pltpu.VMEM((total_rows, hidden_units), BF),
            pltpu.VMEM((total_rows, 128), F32),
            pltpu.VMEM((tp_count, total_rows, features), BF),
            pltpu.SemaphoreType.DMA((4, 3)),
            pltpu.SemaphoreType.DMA((17,)),
        ],
        out_spec=ANY,
        limit=FULL,
        flops=6 * total_rows * hidden_units * features * tp_count,
        moved=24 << 20,
        name="expert",
    )(dp_index, arrived, both, both_core, both_chip, both_far, down, down_core, down_chip, down_far)
    block = -(-(features // 128 * CAP) // 8) * 8

    def weigh(term, ids):
        return call(
            functools.partial(weigh_kernel, term),
            jax.ShapeDtypeStruct((ctx_count, block, features), BF),
            [VMEM] * 2,
            name="weigh",
        )(ids, weight)

    partial, ids_later = lax.optimization_barrier((partial, ids))
    groups = all_to_all(partial, "tp")
    upper, lower = weigh(0, ids_later), weigh(1, ids_later)
    groups, upper, lower = lax.optimization_barrier((groups, upper, lower))
    expert_out = call(
        total_kernel,
        jax.ShapeDtypeStruct((ctx_count, block, 128), BF),
        [VMEM],
        [pltpu.VMEM((total_rows, features), F32)],
        name="total",
    )(groups)
    returned = all_to_all(expert_out, "ctx")
    mixed = call(
        combine_kernel,
        jax.ShapeDtypeStruct((rows, features), BF),
        [VMEM] * 4,
        name="combine",
    )(post, upper, lower, returned)
    return mixed[None]


def solution(mesh):
    placed = (
        P("dp", "ctx", "tp"),
        P("dp", "ctx", "tp"),
        P("dp", "ctx", "tp"),
        P("dp", "ctx"),
        P("dp", "ctx", "tp"),
        P("tp"),
        P("dp", "ctx", None),
        P("dp", "ctx", None),
        P("ctx", "dp", "tp"),
        P("ctx", "dp", "tp"),
        P("ctx", "tp", "dp"),
    )
    return jax.shard_map(
        on_device, mesh=mesh, in_specs=placed, out_specs=P("dp", "ctx", "tp"), check_vma=False
    )
```

```python
import functools
import math

import jax
import jax.numpy as jnp
from jax import lax
from jax.experimental import pallas as pl
from jax.experimental.pallas import tpu as pltpu
from jax.sharding import PartitionSpec as P

HEAD_DIM = 128
CAP = 33
EXPERTS = 16
FULL = 58 << 20
REACH = 1152
BF = jnp.bfloat16
F32 = jnp.float32
VMEM = pl.BlockSpec(memory_space=pltpu.VMEM)
SMEM = pl.BlockSpec(memory_space=pltpu.SMEM)
ANY = pl.BlockSpec(memory_space=pl.ANY)
NN = (((1,), (0,)), ((), ()))
NT = (((1,), (1,)), ((), ()))
TN = (((0,), (0,)), ((), ()))


def dot(a, b, dims=NN):
    return lax.dot_general(a, b, dims, preferred_element_type=F32)


def call(body, out, specs, scratch=(), out_spec=VMEM, limit=32 << 20, flops=0, moved=0, name=None):
    return pl.pallas_call(
        body,
        out_shape=out,
        in_specs=specs,
        out_specs=jax.tree.map(lambda _: out_spec, out),
        scratch_shapes=list(scratch),
        compiler_params=pltpu.CompilerParams(vmem_limit_bytes=limit),
        cost_estimate=pl.CostEstimate(flops=flops, bytes_accessed=moved, transcendentals=0),
        name=name,
    )


def terms(x, count):
    out = []
    for _ in range(count):
        part = x.astype(BF).astype(F32)
        out.append(part)
        x = x - part
    return out


def stack_kernel(gate_ref, up_ref, value_ref, both_ref, rest_ref, held, few, arrive, leave):
    count, rows, _ = rest_ref.shape
    first = pltpu.make_async_copy(value_ref.at[pl.ds(value_ref.shape[0] - rows, rows), :], few, arrive.at[2])
    first.start()
    into = [pltpu.make_async_copy(source, held.at[i], arrive.at[i]) for i, source in enumerate((gate_ref, up_ref))]
    away = [pltpu.make_async_copy(held.at[i], both_ref.at[i], leave.at[i]) for i in range(2)]
    for copy in into:
        copy.start()
    first.wait()
    away += [pltpu.make_async_copy(few, rest_ref.at[i], leave.at[2 + i]) for i in range(count)]
    for copy in away[2:]:
        copy.start()
    for one, then in zip(into, away):
        one.wait()
        then.start()
    for copy in away:
        copy.wait()


def named_and_rank(ids_ref, experts):
    tokens = ids_ref.shape[1]
    expert = lax.broadcasted_iota(jnp.int32, (experts, tokens), 0)
    named = jnp.zeros((experts, tokens), F32)
    for k in range(ids_ref.shape[0]):
        named = named + jnp.where(ids_ref[k : k + 1, :] == expert, 1.0, 0.0)
    before = lax.broadcasted_iota(jnp.int32, (tokens, tokens), 0) < lax.broadcasted_iota(jnp.int32, (tokens, tokens), 1)
    rank = dot(named.astype(BF), jnp.where(before, 1.0, 0.0).astype(BF))
    return jnp.where(named > 0.5, rank, -10000.0)


def attend_kernel(
    back, v_first, place_ref, q_ref, kv_ref, rest_ref, docs_ref, res_ref, ids_ref, post_ref, out_ref, scores
):
    here = place_ref[0]
    rows, wide = q_ref.shape
    group = wide // HEAD_DIM
    scale = 1.0 / math.sqrt(HEAD_DIM)
    q = jnp.concatenate([q_ref[:, g * HEAD_DIM : (g + 1) * HEAD_DIM] for g in range(group)], axis=0)
    own = jnp.concatenate([docs_ref[...]] * group, axis=0)
    low = jnp.maximum(here - back, 0)
    row = lax.rem(lax.broadcasted_iota(jnp.int32, (group * rows, rows), 0), rows)
    col = lax.broadcasted_iota(jnp.int32, (group * rows, rows), 1)
    ahead = col - row
    docs_at = rows + v_first

    def first(j, top):
        s = dot(q, kv_ref[j, 0:rows, :], NT) * scale
        docs = kv_ref[j, docs_at : docs_at + 8, :][0:1, :].astype(F32)
        allowed = (docs == own) & (ahead <= (here - j) * rows)
        s = jnp.where(allowed, s, -1e30)
        scores[j - low] = s
        return jnp.maximum(top, s)

    top = lax.fori_loop(low, here + 1, first, jnp.full((group * rows, rows), -1e30, F32))
    top = jnp.max(top, axis=1, keepdims=True)

    def second(j, carry):
        total, added = carry
        s = scores[j - low]
        w = jnp.where(s > -1e29, jnp.exp(s - top), 0.0)
        values = jnp.concatenate([kv_ref[j, rows : rows + v_first, :], rest_ref[j]], axis=0)
        return total + w, added + dot(w.astype(BF), values)

    zero = jnp.zeros((group * rows, rows), F32)
    total, added = lax.fori_loop(low, here + 1, second, (zero, jnp.zeros((group * rows, HEAD_DIM), F32)))
    attn = (added / jnp.sum(total, axis=1, keepdims=True)).astype(BF).astype(F32)
    attn = jnp.concatenate([attn[g * rows : (g + 1) * rows] for g in range(group)], axis=1)
    post = res_ref[...].astype(F32) + attn
    post_ref[...] = post

    experts, block, lanes = out_ref.shape
    groups = wide // lanes
    mean = jnp.mean(post, axis=1, keepdims=True)
    centred = post - mean
    square = jnp.sum(centred * centred, axis=1, keepdims=True)
    lane = lax.broadcasted_iota(jnp.int32, (rows, lanes), 1)
    stats = jnp.zeros((rows, lanes), F32)
    for q, part in enumerate(terms(mean, 3) + terms(square, 2)):
        stats = jnp.where(lane == q, part, stats)
    source = jnp.concatenate([centred.astype(BF), stats.astype(BF)], axis=1)
    rank = named_and_rank(ids_ref, experts).astype(jnp.int32)
    deep = -(-CAP // 8) * 8
    slot = lax.broadcasted_iota(jnp.int32, (deep, rows), 0)
    picks = [jnp.where(slot == rank[e : e + 1, :], 1.0, 0.0) for e in range(experts)]
    found = dot(jnp.concatenate(picks, axis=0).astype(BF), source)
    turned = found[:, wide:].T[0:8]
    for e in range(experts):
        mine = slice(e * deep, e * deep + CAP)
        runs = [found[mine, g * lanes : (g + 1) * lanes] for g in range(groups)]
        numbers = jnp.concatenate([turned[:, e * deep : (e + 1) * deep], jnp.zeros((8, lanes - deep), F32)], axis=1)
        out_ref[e] = jnp.concatenate(runs + [numbers[: block - groups * CAP]], axis=0).astype(BF)


def spread_kernel(in_ref, gain_ref, out_ref, flat):
    blocks, block, lanes = in_ref.shape
    copies, _, features = out_ref.shape
    groups = features // lanes
    half = blocks // 2
    stats = []
    for b in range(blocks):
        x = in_ref[b].astype(F32)
        for g in range(groups):
            flat[b * CAP : (b + 1) * CAP, g * lanes : (g + 1) * lanes] = x[g * CAP : (g + 1) * CAP]
        stats.append(jnp.concatenate([x[groups * CAP :], jnp.zeros((8 - block + groups * CAP, lanes), F32)], axis=0))
    at = lax.broadcasted_iota(jnp.int32, (half * lanes, features), 0)
    lane = lax.broadcasted_iota(jnp.int32, (half * lanes, features), 1)
    slot = lax.rem(at, lanes)
    put = jnp.where((lane == lax.div(at, lanes) * CAP + slot) & (slot < CAP), 1.0, 0.0).astype(BF)
    top = blocks * CAP
    for h in range(2):
        mine = jnp.concatenate(stats[h * half : (h + 1) * half], axis=1).astype(BF)
        flat[top + 5 * h : top + 5 * h + 5, :] = dot(mine, put)[0:5]
    flat[top + 10 : top + 16, :] = jnp.concatenate(
        terms(gain_ref[...], 3) + [jnp.zeros((3, features), F32)], axis=0
    )
    result = flat[...].astype(BF)
    for c in range(copies):
        out_ref[c] = result


def expert_kernel(
    dp_ref, x_ref, g0, g1, g2, g3, d0, d1, d2, d3, out_ref, x_in, tails, held, gate, up, hidden, column, y_out, sems, more
):
    dp = dp_ref[0]
    parts, total, features = x_ref.shape
    rows = total - 16
    half = rows // 2
    arriving = {("tails",): pltpu.make_async_copy(x_ref.at[:, pl.ds(rows, 16), :], tails, more.at[8])}
    for p in range(4):
        for i in range(2):
            source = x_ref.at[2 * (dp ^ p) + i, pl.ds(0, rows), :]
            arriving["x", p, i] = pltpu.make_async_copy(source, x_in.at[2 * p + i], more.at[2 * p + i])
        for m in range(3):
            source = (d0, d1, d2, d3)[p] if m == 2 else (g0, g1, g2, g3)[p].at[m]
            arriving[p, m] = pltpu.make_async_copy(source, held.at[p, m], sems.at[p, m])

    def begin(*keys):
        for key in keys:
            arriving[key].start()

    def piece(p):
        return ("x", p, 0), ("x", p, 1), (p, 0), (p, 1)

    begin(("tails",), *piece(0))
    arriving["tails",].wait()
    begin(*piece(1))
    means, squares = [], []
    for q in range(parts):
        tail = tails[q].astype(F32)
        means.append([tail[5 * h : 5 * h + 1] + tail[5 * h + 1 : 5 * h + 2] + tail[5 * h + 2 : 5 * h + 3] for h in (0, 1)])
        squares.append([tail[5 * h + 3 : 5 * h + 4] + tail[5 * h + 4 : 5 * h + 5] for h in (0, 1)])
    for h in (0, 1):
        average = sum(m[h] for m in means) / parts
        shifts = [m[h] - average for m in means]
        spread = (sum(s[h] for s in squares) + features * sum(s * s for s in shifts)) / (parts * features)
        block = jnp.concatenate(shifts + [lax.rsqrt(spread + 1e-5), jnp.zeros((128 - parts - 1, features), F32)], axis=0)
        column[h * half : (h + 1) * half, :] = block.T[0:half]

    def normed(p, i):
        q = 2 * (dp ^ p) + i
        tail = tails[q].astype(F32)
        gain = tail[10:11] + tail[11:12] + tail[12:13]
        at = lax.broadcasted_iota(jnp.int32, (rows, 128), 1)
        shift = jnp.sum(jnp.where(at == q, column[...], 0.0), axis=1, keepdims=True)
        scale = column[:, parts : parts + 1]
        arriving["x", p, i].wait()
        return ((x_in[2 * p + i].astype(F32) + shift) * scale * gain).astype(BF)

    for p in range(4):
        x = jnp.concatenate([normed(p, 0), normed(p, 1)], axis=1)
        arriving[p, 0].wait()
        arriving[p, 1].wait()
        if p < 2:
            begin(*piece(p + 2))
        else:
            begin((2 * p - 4, 2), (2 * p - 3, 2))
        g = dot(x, held[p, 0], NT)
        u = dot(x, held[p, 1], NT)
        if p == 0:
            gate[...] = g
            up[...] = u
        elif p < 3:
            gate[...] += g
            up[...] += u
        else:
            g = gate[...] + g
            u = up[...] + u
            hidden[...] = (g / (1.0 + jnp.exp(-g)) * u).astype(BF)
    leaving = []
    for p in range(4):
        j = dp ^ p
        arriving[p, 2].wait()
        y = dot(hidden[...], held[p, 2]).astype(BF)
        for i in range(2):
            y_out[2 * p + i] = y[:, i * features : (i + 1) * features]
            leaving.append(pltpu.make_async_copy(y_out.at[2 * p + i], out_ref.at[2 * j + i], more.at[9 + 2 * p + i]))
            leaving[-1].start()
    for copy in leaving:
        copy.wait()


def total_kernel(in_ref, out_ref, flat):
    parts, _, features = in_ref.shape
    blocks, rows, lanes = out_ref.shape
    total = in_ref[0].astype(F32)
    for p in range(1, parts):
        total = total + in_ref[p].astype(F32)
    flat[0 : total.shape[0], :] = total
    groups = features // lanes
    for b in range(blocks):
        block = flat[b * CAP : (b + 1) * CAP, :]
        runs = [block[:, g * lanes : (g + 1) * lanes] for g in range(groups)]
        runs.append(jnp.zeros((rows - groups * CAP, lanes), F32))
        out_ref[b] = jnp.concatenate(runs, axis=0).astype(BF)


def weigh_kernel(term, ids_ref, weight_ref, out_ref):
    wide, places = out_ref.shape
    tokens = ids_ref.shape[1]
    groups = wide // tokens
    experts = EXPERTS
    block = places // experts
    rank = named_and_rank(ids_ref, experts)
    expert = lax.broadcasted_iota(jnp.int32, (experts, tokens), 0)
    weight = jnp.zeros((experts, tokens), F32)
    for k in range(ids_ref.shape[0]):
        weight = weight + jnp.where(ids_ref[k : k + 1, :] == expert, weight_ref[k : k + 1, :], 0.0)
    weight = terms(weight, 2)[term]
    place = lax.broadcasted_iota(jnp.int32, (experts, places), 1)
    start = lax.broadcasted_iota(jnp.int32, (experts, places), 0) * block
    own = jnp.where((place >= start) & (place < start + block), 1.0, 0.0).astype(BF)
    rank = dot(rank.astype(BF), own, TN)
    weight = dot(weight.astype(BF), own, TN)
    at = lax.rem(lax.broadcasted_iota(jnp.int32, (tokens, places), 1), block).astype(F32)
    for g in range(groups):
        out_ref[g * tokens : (g + 1) * tokens, :] = jnp.where(at == rank + g * CAP, weight, 0.0).astype(BF)


def combine_kernel(post_ref, upper_ref, lower_ref, back_ref, out_ref):
    tokens, features = post_ref.shape
    groups = features // back_ref.shape[1]
    back = back_ref[...]
    moe = dot(upper_ref[...], back) + dot(lower_ref[...], back)
    moe = jnp.concatenate([moe[g * tokens : (g + 1) * tokens] for g in range(groups)], axis=1)
    out_ref[...] = (post_ref[...] + moe).astype(BF)


def all_to_all(x, axis):
    return lax.all_to_all(x, axis, split_axis=0, concat_axis=0, tiled=True)


def on_device(
    queries,
    key_heads,
    value_heads,
    doc_ids,
    residual,
    ln_gain,
    expert_ids,
    expert_weight,
    w_gate,
    w_up,
    w_down,
):
    rows = queries.shape[1]
    features = residual.shape[2]
    ctx_count = lax.axis_size("ctx")
    tp_count = lax.axis_size("tp")
    dp_index = lax.axis_index("dp").reshape(1)
    ctx_index = lax.axis_index("ctx").reshape(1)
    ids = expert_ids[0].T
    weight = expert_weight[0].T
    hidden_units = w_down.shape[1]

    other_chip = [(i, i ^ 2) for i in range(4)]
    other_core = [(i, i ^ 1) for i in range(4)]
    down = w_down[0]
    v_first = rows - 16
    both, rest = call(
        stack_kernel,
        (
            jax.ShapeDtypeStruct((2,) + down.shape, BF),
            jax.ShapeDtypeStruct((ctx_count, rows - v_first, HEAD_DIM), BF),
        ),
        [ANY] * 3,
        [
            pltpu.VMEM((2,) + down.shape, BF),
            pltpu.VMEM((rows - v_first, HEAD_DIM), BF),
            pltpu.SemaphoreType.DMA((3,)),
            pltpu.SemaphoreType.DMA((2 + ctx_count,)),
        ],
        out_spec=ANY,
        limit=FULL,
        name="stack",
    )(w_gate[0].T, w_up[0].T, value_heads[0])
    both_chip = lax.ppermute(both, "dp", other_chip)

    docs_row = jnp.broadcast_to(doc_ids.astype(BF), (8, rows))
    packed = jnp.concatenate([key_heads[0], value_heads[0, :v_first], docs_row], axis=0)
    rest = all_to_all(rest, "ctx")
    kv = lax.all_gather(packed, "ctx", axis=0)
    back = -(-(REACH - 1) // rows)
    group = queries.shape[2] // HEAD_DIM
    block = -(-(features // 128 * CAP + 5) // 8) * 8
    post, outgoing = call(
        functools.partial(attend_kernel, back, v_first),
        (jax.ShapeDtypeStruct((rows, features), F32), jax.ShapeDtypeStruct((ctx_count, block, 128), BF)),
        [SMEM] + [VMEM] * 6,
        [pltpu.VMEM((back + 1, group * rows, rows), F32)],
        name="attend",
    )(ctx_index, queries[0], kv, rest, doc_ids[0].astype(F32).reshape(rows, 1), residual[0], ids)
    outgoing, down, both, both_chip = lax.optimization_barrier((outgoing, down, both, both_chip))
    landed = all_to_all(outgoing, "ctx")
    down_chip = lax.ppermute(down, "dp", other_chip)
    both_core = lax.ppermute(both, "dp", other_core)
    both_far = lax.ppermute(both_chip, "dp", other_core)
    down_core = lax.ppermute(down, "dp", other_core)
    total_rows = ctx_count * CAP
    copies = call(
        spread_kernel,
        jax.ShapeDtypeStruct((tp_count, total_rows + 16, features), BF),
        [VMEM] * 2,
        [pltpu.VMEM((total_rows + 16, features), F32)],
        name="spread",
    )(landed, ln_gain.reshape(1, features))
    copies, down_chip = lax.optimization_barrier((copies, down_chip))
    arrived = all_to_all(copies, "tp")
    down_far = lax.ppermute(down_chip, "dp", other_core)
    partial = call(
        expert_kernel,
        jax.ShapeDtypeStruct((tp_count, total_rows, features), BF),
        [SMEM] + [ANY] * 9,
        [
            pltpu.VMEM((tp_count, total_rows, features), BF),
            pltpu.VMEM((tp_count, 16, features), BF),
            pltpu.VMEM((4, 3) + down.shape, BF),
            pltpu.VMEM((total_rows, hidden_units), F32),
            pltpu.VMEM((total_rows, hidden_units), F32),
            pltpu.VMEM((total_rows, hidden_units), BF),
            pltpu.VMEM((total_rows, 128), F32),
            pltpu.VMEM((tp_count, total_rows, features), BF),
            pltpu.SemaphoreType.DMA((4, 3)),
            pltpu.SemaphoreType.DMA((17,)),
        ],
        out_spec=ANY,
        limit=FULL,
        flops=6 * total_rows * hidden_units * features * tp_count,
        moved=24 << 20,
        name="expert",
    )(dp_index, arrived, both, both_core, both_chip, both_far, down, down_core, down_chip, down_far)
    block = -(-(features // 128 * CAP) // 8) * 8

    def weigh(term, ids):
        return call(
            functools.partial(weigh_kernel, term),
            jax.ShapeDtypeStruct((features, ctx_count * block), BF),
            [VMEM] * 2,
            name="weigh",
        )(ids, weight)

    partial, ids_later = lax.optimization_barrier((partial, ids))
    groups = all_to_all(partial, "tp")
    upper, lower = weigh(0, ids_later), weigh(1, ids_later)
    groups, upper, lower = lax.optimization_barrier((groups, upper, lower))
    expert_out = call(
        total_kernel,
        jax.ShapeDtypeStruct((ctx_count, block, 128), BF),
        [VMEM],
        [pltpu.VMEM((total_rows + 16, features), F32)],
        name="total",
    )(groups)
    returned = all_to_all(expert_out, "ctx")
    mixed = call(
        combine_kernel,
        jax.ShapeDtypeStruct((rows, features), BF),
        [VMEM] * 4,
        name="combine",
    )(post, upper, lower, returned.reshape(ctx_count * block, 128))
    return mixed[None]


def solution(mesh):
    placed = (
        P("dp", "ctx", "tp"),
        P("dp", "ctx", "tp"),
        P("dp", "ctx", "tp"),
        P("dp", "ctx"),
        P("dp", "ctx", "tp"),
        P("tp"),
        P("dp", "ctx", None),
        P("dp", "ctx", None),
        P("ctx", "dp", "tp"),
        P("ctx", "dp", "tp"),
        P("ctx", "tp", "dp"),
    )
    return jax.shard_map(
        on_device, mesh=mesh, in_specs=placed, out_specs=P("dp", "ctx", "tp"), check_vma=False
    )
```

```python
import functools
import math

import jax
import jax.numpy as jnp
from jax import lax
from jax.experimental import pallas as pl
from jax.experimental.pallas import tpu as pltpu
from jax.sharding import PartitionSpec as P

HEAD_DIM = 128
CAP = 33
EXPERTS = 16
FULL = 58 << 20
REACH = 1152
BF = jnp.bfloat16
F32 = jnp.float32
VMEM = pl.BlockSpec(memory_space=pltpu.VMEM)
SMEM = pl.BlockSpec(memory_space=pltpu.SMEM)
ANY = pl.BlockSpec(memory_space=pl.ANY)
NN = (((1,), (0,)), ((), ()))
NT = (((1,), (1,)), ((), ()))
TN = (((0,), (0,)), ((), ()))


def dot(a, b, dims=NN):
    return lax.dot_general(a, b, dims, preferred_element_type=F32)


def call(body, out, specs, scratch=(), out_spec=VMEM, limit=32 << 20, flops=0, moved=0, name=None):
    return pl.pallas_call(
        body,
        out_shape=out,
        in_specs=specs,
        out_specs=jax.tree.map(lambda _: out_spec, out),
        scratch_shapes=list(scratch),
        compiler_params=pltpu.CompilerParams(vmem_limit_bytes=limit),
        cost_estimate=pl.CostEstimate(flops=flops, bytes_accessed=moved, transcendentals=0),
        name=name,
    )


def terms(x, count):
    out = []
    for _ in range(count):
        part = x.astype(BF).astype(F32)
        out.append(part)
        x = x - part
    return out


def stack_kernel(gate_ref, up_ref, value_ref, both_ref, rest_ref, held, few, arrive, leave):
    count, rows, _ = rest_ref.shape
    first = pltpu.make_async_copy(value_ref.at[pl.ds(value_ref.shape[0] - rows, rows), :], few, arrive.at[2])
    first.start()
    into = [pltpu.make_async_copy(source, held.at[i], arrive.at[i]) for i, source in enumerate((gate_ref, up_ref))]
    away = [pltpu.make_async_copy(held.at[i], both_ref.at[i], leave.at[i]) for i in range(2)]
    for copy in into:
        copy.start()
    first.wait()
    away += [pltpu.make_async_copy(few, rest_ref.at[i], leave.at[2 + i]) for i in range(count)]
    for copy in away[2:]:
        copy.start()
    for one, then in zip(into, away):
        one.wait()
        then.start()
    for copy in away:
        copy.wait()


def named_and_rank(ids_ref, experts):
    tokens = ids_ref.shape[1]
    expert = lax.broadcasted_iota(jnp.int32, (experts, tokens), 0)
    named = jnp.zeros((experts, tokens), F32)
    for k in range(ids_ref.shape[0]):
        named = named + jnp.where(ids_ref[k : k + 1, :] == expert, 1.0, 0.0)
    before = lax.broadcasted_iota(jnp.int32, (tokens, tokens), 0) < lax.broadcasted_iota(jnp.int32, (tokens, tokens), 1)
    rank = dot(named.astype(BF), jnp.where(before, 1.0, 0.0).astype(BF))
    return jnp.where(named > 0.5, rank, -10000.0)


def attend_kernel(
    back, v_first, place_ref, q_ref, kv_ref, rest_ref, docs_ref, res_ref, ids_ref, post_ref, out_ref, scores
):
    here = place_ref[0]
    rows, wide = q_ref.shape
    group = wide // HEAD_DIM
    scale = 1.0 / math.sqrt(HEAD_DIM)
    q = jnp.concatenate([q_ref[:, g * HEAD_DIM : (g + 1) * HEAD_DIM] for g in range(group)], axis=0)
    own = jnp.concatenate([docs_ref[...]] * group, axis=0)
    low = jnp.maximum(here - back, 0)
    row = lax.rem(lax.broadcasted_iota(jnp.int32, (group * rows, rows), 0), rows)
    col = lax.broadcasted_iota(jnp.int32, (group * rows, rows), 1)
    ahead = col - row
    docs_at = rows + v_first

    def first(j, top):
        s = dot(q, kv_ref[j, 0:rows, :], NT) * scale
        docs = kv_ref[j, docs_at : docs_at + 8, :][0:1, :].astype(F32)
        allowed = (docs == own) & (ahead <= (here - j) * rows)
        s = jnp.where(allowed, s, -1e30)
        scores[j - low] = s
        return jnp.maximum(top, s)

    top = lax.fori_loop(low, here + 1, first, jnp.full((group * rows, rows), -1e30, F32))
    top = jnp.max(top, axis=1, keepdims=True)

    def second(j, carry):
        total, added = carry
        s = scores[j - low]
        w = jnp.where(s > -1e29, jnp.exp(s - top), 0.0)
        values = jnp.concatenate([kv_ref[j, rows : rows + v_first, :], rest_ref[j]], axis=0)
        return total + w, added + dot(w.astype(BF), values)

    zero = jnp.zeros((group * rows, rows), F32)
    total, added = lax.fori_loop(low, here + 1, second, (zero, jnp.zeros((group * rows, HEAD_DIM), F32)))
    attn = (added / jnp.sum(total, axis=1, keepdims=True)).astype(BF).astype(F32)
    attn = jnp.concatenate([attn[g * rows : (g + 1) * rows] for g in range(group)], axis=1)
    post = res_ref[...].astype(F32) + attn
    post_ref[...] = post

    experts, block, lanes = out_ref.shape
    groups = wide // lanes
    mean = jnp.mean(post, axis=1, keepdims=True)
    centred = post - mean
    square = jnp.sum(centred * centred, axis=1, keepdims=True)
    lane = lax.broadcasted_iota(jnp.int32, (rows, lanes), 1)
    stats = jnp.zeros((rows, lanes), F32)
    for q, part in enumerate(terms(mean, 3) + terms(square, 2)):
        stats = jnp.where(lane == q, part, stats)
    source = jnp.concatenate([centred.astype(BF), stats.astype(BF)], axis=1)
    rank = named_and_rank(ids_ref, experts).astype(jnp.int32)
    deep = -(-CAP // 8) * 8
    slot = lax.broadcasted_iota(jnp.int32, (deep, rows), 0)
    picks = [jnp.where(slot == rank[e : e + 1, :], 1.0, 0.0) for e in range(experts)]
    found = dot(jnp.concatenate(picks, axis=0).astype(BF), source)
    turned = found[:, wide:].T[0:8]
    for e in range(experts):
        mine = slice(e * deep, e * deep + CAP)
        runs = [found[mine, g * lanes : (g + 1) * lanes] for g in range(groups)]
        numbers = jnp.concatenate([turned[:, e * deep : (e + 1) * deep], jnp.zeros((8, lanes - deep), F32)], axis=1)
        out_ref[e] = jnp.concatenate(runs + [numbers[: block - groups * CAP]], axis=0).astype(BF)


def spread_kernel(in_ref, gain_ref, out_ref, flat):
    blocks, block, lanes = in_ref.shape
    copies, _, features = out_ref.shape
    groups = features // lanes
    half = blocks // 2
    stats = []
    for b in range(blocks):
        x = in_ref[b].astype(F32)
        for g in range(groups):
            flat[b * CAP : (b + 1) * CAP, g * lanes : (g + 1) * lanes] = x[g * CAP : (g + 1) * CAP]
        stats.append(jnp.concatenate([x[groups * CAP :], jnp.zeros((8 - block + groups * CAP, lanes), F32)], axis=0))
    at = lax.broadcasted_iota(jnp.int32, (half * lanes, features), 0)
    lane = lax.broadcasted_iota(jnp.int32, (half * lanes, features), 1)
    slot = lax.rem(at, lanes)
    put = jnp.where((lane == lax.div(at, lanes) * CAP + slot) & (slot < CAP), 1.0, 0.0).astype(BF)
    top = blocks * CAP
    for h in range(2):
        mine = jnp.concatenate(stats[h * half : (h + 1) * half], axis=1).astype(BF)
        flat[top + 5 * h : top + 5 * h + 5, :] = dot(mine, put)[0:5]
    flat[top + 10 : top + 16, :] = jnp.concatenate(
        terms(gain_ref[...], 3) + [jnp.zeros((3, features), F32)], axis=0
    )
    result = flat[...].astype(BF)
    for c in range(copies):
        out_ref[c] = result


def expert_kernel(
    dp_ref, x_ref, g0, g1, g2, g3, d0, d1, d2, d3, out_ref, x_in, tails, held, gate, up, hidden, column, y_out, sems, more
):
    dp = dp_ref[0]
    parts, total, features = x_ref.shape
    rows = total - 16
    half = rows // 2
    arriving = {("tails",): pltpu.make_async_copy(x_ref.at[:, pl.ds(rows, 16), :], tails, more.at[8])}
    for p in range(4):
        for i in range(2):
            source = x_ref.at[2 * (dp ^ p) + i, pl.ds(0, rows), :]
            arriving["x", p, i] = pltpu.make_async_copy(source, x_in.at[2 * p + i], more.at[2 * p + i])
        for m in range(3):
            source = (d0, d1, d2, d3)[p] if m == 2 else (g0, g1, g2, g3)[p].at[m]
            arriving[p, m] = pltpu.make_async_copy(source, held.at[p, m], sems.at[p, m])

    def begin(*keys):
        for key in keys:
            arriving[key].start()

    def piece(p):
        return ("x", p, 0), ("x", p, 1), (p, 0), (p, 1)

    begin(("tails",), *piece(0))
    arriving["tails",].wait()
    begin(*piece(1))
    means, squares = [], []
    for q in range(parts):
        tail = tails[q].astype(F32)
        means.append([tail[5 * h : 5 * h + 1] + tail[5 * h + 1 : 5 * h + 2] + tail[5 * h + 2 : 5 * h + 3] for h in (0, 1)])
        squares.append([tail[5 * h + 3 : 5 * h + 4] + tail[5 * h + 4 : 5 * h + 5] for h in (0, 1)])
    for h in (0, 1):
        average = sum(m[h] for m in means) / parts
        shifts = [m[h] - average for m in means]
        spread = (sum(s[h] for s in squares) + features * sum(s * s for s in shifts)) / (parts * features)
        block = jnp.concatenate(shifts + [lax.rsqrt(spread + 1e-5), jnp.zeros((128 - parts - 1, features), F32)], axis=0)
        column[h * half : (h + 1) * half, :] = block.T[0:half]

    def normed(p, i):
        q = 2 * (dp ^ p) + i
        tail = tails[q].astype(F32)
        gain = tail[10:11] + tail[11:12] + tail[12:13]
        at = lax.broadcasted_iota(jnp.int32, (rows, 128), 1)
        shift = jnp.sum(jnp.where(at == q, column[...], 0.0), axis=1, keepdims=True)
        scale = column[:, parts : parts + 1]
        arriving["x", p, i].wait()
        return ((x_in[2 * p + i].astype(F32) + shift) * scale * gain).astype(BF)

    for now in ((0,), (1,), (2, 3)):
        x = [jnp.concatenate([normed(p, 0), normed(p, 1)], axis=1) for p in now]
        for p in now:
            arriving[p, 0].wait()
            arriving[p, 1].wait()
        if now[0] < 2:
            begin(*piece(now[0] + 2))
        if now[0] > 0:
            begin((2 * now[0] - 2, 2), (2 * now[0] - 1, 2))
        g = sum(dot(part, held[p, 0], NT) for p, part in zip(now, x))
        u = sum(dot(part, held[p, 1], NT) for p, part in zip(now, x))
        if now[0] == 0:
            gate[...] = g
            up[...] = u
        elif now[0] < 2:
            gate[...] += g
            up[...] += u
        else:
            g = gate[...] + g
            u = up[...] + u
            hidden[...] = (g / (1.0 + jnp.exp(-g)) * u).astype(BF)
    leaving = []
    for p in range(4):
        arriving[p, 2].wait()
    for now in ((0, 1), (2, 3)):
        for p in now:
            y = dot(hidden[...], held[p, 2]).astype(BF)
            for i in range(2):
                y_out[2 * p + i] = y[:, i * features : (i + 1) * features]
        for p in now:
            for i in range(2):
                target = out_ref.at[2 * (dp ^ p) + i]
                leaving.append(pltpu.make_async_copy(y_out.at[2 * p + i], target, more.at[9 + 2 * p + i]))
                leaving[-1].start()
    for copy in leaving:
        copy.wait()


def total_kernel(in_ref, out_ref, flat):
    parts, _, features = in_ref.shape
    blocks, rows, lanes = out_ref.shape
    total = in_ref[0].astype(F32)
    for p in range(1, parts):
        total = total + in_ref[p].astype(F32)
    flat[0 : total.shape[0], :] = total
    groups = features // lanes
    for b in range(blocks):
        block = flat[b * CAP : (b + 1) * CAP, :]
        runs = [block[:, g * lanes : (g + 1) * lanes] for g in range(groups)]
        runs.append(jnp.zeros((rows - groups * CAP, lanes), F32))
        out_ref[b] = jnp.concatenate(runs, axis=0).astype(BF)


def weigh_kernel(term, ids_ref, weight_ref, out_ref):
    wide, places = out_ref.shape
    tokens = ids_ref.shape[1]
    groups = wide // tokens
    experts = EXPERTS
    block = places // experts
    rank = named_and_rank(ids_ref, experts)
    expert = lax.broadcasted_iota(jnp.int32, (experts, tokens), 0)
    weight = jnp.zeros((experts, tokens), F32)
    for k in range(ids_ref.shape[0]):
        weight = weight + jnp.where(ids_ref[k : k + 1, :] == expert, weight_ref[k : k + 1, :], 0.0)
    weight = terms(weight, 2)[term]
    place = lax.broadcasted_iota(jnp.int32, (experts, places), 1)
    start = lax.broadcasted_iota(jnp.int32, (experts, places), 0) * block
    own = jnp.where((place >= start) & (place < start + block), 1.0, 0.0).astype(BF)
    rank = dot(rank.astype(BF), own, TN)
    weight = dot(weight.astype(BF), own, TN)
    at = lax.rem(lax.broadcasted_iota(jnp.int32, (tokens, places), 1), block).astype(F32)
    for g in range(groups):
        out_ref[g * tokens : (g + 1) * tokens, :] = jnp.where(at == rank + g * CAP, weight, 0.0).astype(BF)


def combine_kernel(post_ref, upper_ref, lower_ref, back_ref, out_ref):
    tokens, features = post_ref.shape
    groups = features // back_ref.shape[1]
    back = back_ref[...]
    moe = dot(upper_ref[...], back) + dot(lower_ref[...], back)
    moe = jnp.concatenate([moe[g * tokens : (g + 1) * tokens] for g in range(groups)], axis=1)
    out_ref[...] = (post_ref[...] + moe).astype(BF)


def all_to_all(x, axis):
    return lax.all_to_all(x, axis, split_axis=0, concat_axis=0, tiled=True)


def on_device(
    queries,
    key_heads,
    value_heads,
    doc_ids,
    residual,
    ln_gain,
    expert_ids,
    expert_weight,
    w_gate,
    w_up,
    w_down,
):
    rows = queries.shape[1]
    features = residual.shape[2]
    ctx_count = lax.axis_size("ctx")
    tp_count = lax.axis_size("tp")
    dp_index = lax.axis_index("dp").reshape(1)
    ctx_index = lax.axis_index("ctx").reshape(1)
    ids = expert_ids[0].T
    weight = expert_weight[0].T
    hidden_units = w_down.shape[1]

    other_chip = [(i, i ^ 2) for i in range(4)]
    other_core = [(i, i ^ 1) for i in range(4)]
    down = w_down[0]
    v_first = rows - 16
    both, rest = call(
        stack_kernel,
        (
            jax.ShapeDtypeStruct((2,) + down.shape, BF),
            jax.ShapeDtypeStruct((ctx_count, rows - v_first, HEAD_DIM), BF),
        ),
        [ANY] * 3,
        [
            pltpu.VMEM((2,) + down.shape, BF),
            pltpu.VMEM((rows - v_first, HEAD_DIM), BF),
            pltpu.SemaphoreType.DMA((3,)),
            pltpu.SemaphoreType.DMA((2 + ctx_count,)),
        ],
        out_spec=ANY,
        limit=FULL,
        name="stack",
    )(w_gate[0].T, w_up[0].T, value_heads[0])
    both_chip = lax.ppermute(both, "dp", other_chip)

    docs_row = jnp.broadcast_to(doc_ids.astype(BF), (8, rows))
    packed = jnp.concatenate([key_heads[0], value_heads[0, :v_first], docs_row], axis=0)
    rest = all_to_all(rest, "ctx")
    kv = lax.all_gather(packed, "ctx", axis=0)
    back = -(-(REACH - 1) // rows)
    group = queries.shape[2] // HEAD_DIM
    block = -(-(features // 128 * CAP + 5) // 8) * 8
    post, outgoing = call(
        functools.partial(attend_kernel, back, v_first),
        (jax.ShapeDtypeStruct((rows, features), F32), jax.ShapeDtypeStruct((ctx_count, block, 128), BF)),
        [SMEM] + [VMEM] * 6,
        [pltpu.VMEM((back + 1, group * rows, rows), F32)],
        name="attend",
    )(ctx_index, queries[0], kv, rest, doc_ids[0].astype(F32).reshape(rows, 1), residual[0], ids)
    outgoing, down, both, both_chip = lax.optimization_barrier((outgoing, down, both, both_chip))
    landed = all_to_all(outgoing, "ctx")
    down_chip = lax.ppermute(down, "dp", other_chip)
    both_core = lax.ppermute(both, "dp", other_core)
    both_far = lax.ppermute(both_chip, "dp", other_core)
    down_core = lax.ppermute(down, "dp", other_core)
    total_rows = ctx_count * CAP
    copies = call(
        spread_kernel,
        jax.ShapeDtypeStruct((tp_count, total_rows + 16, features), BF),
        [VMEM] * 2,
        [pltpu.VMEM((total_rows + 16, features), F32)],
        name="spread",
    )(landed, ln_gain.reshape(1, features))
    copies, down_chip = lax.optimization_barrier((copies, down_chip))
    arrived = all_to_all(copies, "tp")
    down_far = lax.ppermute(down_chip, "dp", other_core)
    partial = call(
        expert_kernel,
        jax.ShapeDtypeStruct((tp_count, total_rows, features), BF),
        [SMEM] + [ANY] * 9,
        [
            pltpu.VMEM((tp_count, total_rows, features), BF),
            pltpu.VMEM((tp_count, 16, features), BF),
            pltpu.VMEM((4, 3) + down.shape, BF),
            pltpu.VMEM((total_rows, hidden_units), F32),
            pltpu.VMEM((total_rows, hidden_units), F32),
            pltpu.VMEM((total_rows, hidden_units), BF),
            pltpu.VMEM((total_rows, 128), F32),
            pltpu.VMEM((tp_count, total_rows, features), BF),
            pltpu.SemaphoreType.DMA((4, 3)),
            pltpu.SemaphoreType.DMA((17,)),
        ],
        out_spec=ANY,
        limit=FULL,
        flops=6 * total_rows * hidden_units * features * tp_count,
        moved=24 << 20,
        name="expert",
    )(dp_index, arrived, both, both_core, both_chip, both_far, down, down_core, down_chip, down_far)
    block = -(-(features // 128 * CAP) // 8) * 8

    def weigh(term, ids):
        return call(
            functools.partial(weigh_kernel, term),
            jax.ShapeDtypeStruct((features, ctx_count * block), BF),
            [VMEM] * 2,
            name="weigh",
        )(ids, weight)

    partial, ids_later = lax.optimization_barrier((partial, ids))
    groups = all_to_all(partial, "tp")
    upper, lower = weigh(0, ids_later), weigh(1, ids_later)
    groups, upper, lower = lax.optimization_barrier((groups, upper, lower))
    expert_out = call(
        total_kernel,
        jax.ShapeDtypeStruct((ctx_count, block, 128), BF),
        [VMEM],
        [pltpu.VMEM((total_rows + 16, features), F32)],
        name="total",
    )(groups)
    returned = all_to_all(expert_out, "ctx")
    mixed = call(
        combine_kernel,
        jax.ShapeDtypeStruct((rows, features), BF),
        [VMEM] * 4,
        name="combine",
    )(post, upper, lower, returned.reshape(ctx_count * block, 128))
    return mixed[None]


def solution(mesh):
    placed = (
        P("dp", "ctx", "tp"),
        P("dp", "ctx", "tp"),
        P("dp", "ctx", "tp"),
        P("dp", "ctx"),
        P("dp", "ctx", "tp"),
        P("tp"),
        P("dp", "ctx", None),
        P("dp", "ctx", None),
        P("ctx", "dp", "tp"),
        P("ctx", "dp", "tp"),
        P("ctx", "tp", "dp"),
    )
    return jax.shard_map(
        on_device, mesh=mesh, in_specs=placed, out_specs=P("dp", "ctx", "tp"), check_vma=False
    )
```

```python
import functools
import math

import jax
import jax.numpy as jnp
from jax import lax
from jax.experimental import pallas as pl
from jax.experimental.pallas import tpu as pltpu
from jax.sharding import PartitionSpec as P

HEAD_DIM = 128
CAP = 33
EXPERTS = 16
FULL = 58 << 20
REACH = 1152
BF = jnp.bfloat16
F32 = jnp.float32
VMEM = pl.BlockSpec(memory_space=pltpu.VMEM)
SMEM = pl.BlockSpec(memory_space=pltpu.SMEM)
ANY = pl.BlockSpec(memory_space=pl.ANY)
NN = (((1,), (0,)), ((), ()))
NT = (((1,), (1,)), ((), ()))
TN = (((0,), (0,)), ((), ()))


def dot(a, b, dims=NN):
    return lax.dot_general(a, b, dims, preferred_element_type=F32)


def call(body, out, specs, scratch=(), out_spec=VMEM, limit=32 << 20, flops=0, moved=0, name=None):
    return pl.pallas_call(
        body,
        out_shape=out,
        in_specs=specs,
        out_specs=jax.tree.map(lambda _: out_spec, out),
        scratch_shapes=list(scratch),
        compiler_params=pltpu.CompilerParams(vmem_limit_bytes=limit),
        cost_estimate=pl.CostEstimate(flops=flops, bytes_accessed=moved, transcendentals=0),
        name=name,
    )


def terms(x, count):
    out = []
    for _ in range(count):
        part = x.astype(BF).astype(F32)
        out.append(part)
        x = x - part
    return out


def stack_kernel(gate_ref, up_ref, value_ref, both_ref, rest_ref, held, few, arrive, leave):
    count, rows, _ = rest_ref.shape
    first = pltpu.make_async_copy(value_ref.at[pl.ds(value_ref.shape[0] - rows, rows), :], few, arrive.at[2])
    first.start()
    into = [pltpu.make_async_copy(source, held.at[i], arrive.at[i]) for i, source in enumerate((gate_ref, up_ref))]
    away = [pltpu.make_async_copy(held.at[i], both_ref.at[i], leave.at[i]) for i in range(2)]
    for copy in into:
        copy.start()
    first.wait()
    away += [pltpu.make_async_copy(few, rest_ref.at[i], leave.at[2 + i]) for i in range(count)]
    for copy in away[2:]:
        copy.start()
    for one, then in zip(into, away):
        one.wait()
        then.start()
    for copy in away:
        copy.wait()


def named_and_rank(ids_ref, experts):
    tokens = ids_ref.shape[1]
    expert = lax.broadcasted_iota(jnp.int32, (experts, tokens), 0)
    named = jnp.zeros((experts, tokens), F32)
    for k in range(ids_ref.shape[0]):
        named = named + jnp.where(ids_ref[k : k + 1, :] == expert, 1.0, 0.0)
    before = lax.broadcasted_iota(jnp.int32, (tokens, tokens), 0) < lax.broadcasted_iota(jnp.int32, (tokens, tokens), 1)
    rank = dot(named.astype(BF), jnp.where(before, 1.0, 0.0).astype(BF))
    return jnp.where(named > 0.5, rank, -10000.0)


def attend_kernel(
    back, v_first, place_ref, q_ref, kv_ref, rest_ref, docs_ref, res_ref, ids_ref, post_ref, out_ref, scores
):
    here = place_ref[0]
    rows, wide = q_ref.shape
    group = wide // HEAD_DIM
    scale = 1.0 / math.sqrt(HEAD_DIM)
    q = jnp.concatenate([q_ref[:, g * HEAD_DIM : (g + 1) * HEAD_DIM] for g in range(group)], axis=0)
    own = jnp.concatenate([docs_ref[...]] * group, axis=0)
    low = jnp.maximum(here - back, 0)
    row = lax.rem(lax.broadcasted_iota(jnp.int32, (group * rows, rows), 0), rows)
    col = lax.broadcasted_iota(jnp.int32, (group * rows, rows), 1)
    ahead = col - row
    docs_at = rows + v_first

    def first(j, top):
        s = dot(q, kv_ref[j, 0:rows, :], NT) * scale
        docs = kv_ref[j, docs_at : docs_at + 8, :][0:1, :].astype(F32)
        allowed = (docs == own) & (ahead <= (here - j) * rows)
        s = jnp.where(allowed, s, -1e30)
        scores[j - low] = s
        return jnp.maximum(top, s)

    top = lax.fori_loop(low, here + 1, first, jnp.full((group * rows, rows), -1e30, F32))
    top = jnp.max(top, axis=1, keepdims=True)

    def second(j, carry):
        total, added = carry
        s = scores[j - low]
        w = jnp.where(s > -1e29, jnp.exp(s - top), 0.0)
        values = jnp.concatenate([kv_ref[j, rows : rows + v_first, :], rest_ref[j]], axis=0)
        return total + w, added + dot(w.astype(BF), values)

    zero = jnp.zeros((group * rows, rows), F32)
    total, added = lax.fori_loop(low, here + 1, second, (zero, jnp.zeros((group * rows, HEAD_DIM), F32)))
    attn = (added / jnp.sum(total, axis=1, keepdims=True)).astype(BF).astype(F32)
    attn = jnp.concatenate([attn[g * rows : (g + 1) * rows] for g in range(group)], axis=1)
    post = res_ref[...].astype(F32) + attn
    post_ref[...] = post

    experts, block, lanes = out_ref.shape
    groups = wide // lanes
    mean = jnp.mean(post, axis=1, keepdims=True)
    centred = post - mean
    square = jnp.sum(centred * centred, axis=1, keepdims=True)
    lane = lax.broadcasted_iota(jnp.int32, (rows, lanes), 1)
    stats = jnp.zeros((rows, lanes), F32)
    for q, part in enumerate(terms(mean, 3) + terms(square, 2)):
        stats = jnp.where(lane == q, part, stats)
    source = jnp.concatenate([centred.astype(BF), stats.astype(BF)], axis=1)
    rank = named_and_rank(ids_ref, experts).astype(jnp.int32)
    deep = -(-CAP // 8) * 8
    slot = lax.broadcasted_iota(jnp.int32, (deep, rows), 0)
    picks = [jnp.where(slot == rank[e : e + 1, :], 1.0, 0.0) for e in range(experts)]
    found = dot(jnp.concatenate(picks, axis=0).astype(BF), source)
    turned = found[:, wide:].T[0:8]
    for e in range(experts):
        mine = slice(e * deep, e * deep + CAP)
        runs = [found[mine, g * lanes : (g + 1) * lanes] for g in range(groups)]
        numbers = jnp.concatenate([turned[:, e * deep : (e + 1) * deep], jnp.zeros((8, lanes - deep), F32)], axis=1)
        out_ref[e] = jnp.concatenate(runs + [numbers[: block - groups * CAP]], axis=0).astype(BF)


def spread_kernel(in_ref, gain_ref, out_ref, flat):
    blocks, block, lanes = in_ref.shape
    copies, _, features = out_ref.shape
    groups = features // lanes
    half = blocks // 2
    stats = []
    for b in range(blocks):
        x = in_ref[b].astype(F32)
        for g in range(groups):
            flat[b * CAP : (b + 1) * CAP, g * lanes : (g + 1) * lanes] = x[g * CAP : (g + 1) * CAP]
        stats.append(jnp.concatenate([x[groups * CAP :], jnp.zeros((8 - block + groups * CAP, lanes), F32)], axis=0))
    at = lax.broadcasted_iota(jnp.int32, (half * lanes, features), 0)
    lane = lax.broadcasted_iota(jnp.int32, (half * lanes, features), 1)
    slot = lax.rem(at, lanes)
    put = jnp.where((lane == lax.div(at, lanes) * CAP + slot) & (slot < CAP), 1.0, 0.0).astype(BF)
    top = blocks * CAP
    for h in range(2):
        mine = jnp.concatenate(stats[h * half : (h + 1) * half], axis=1).astype(BF)
        flat[top + 5 * h : top + 5 * h + 5, :] = dot(mine, put)[0:5]
    flat[top + 10 : top + 16, :] = jnp.concatenate(
        terms(gain_ref[...], 3) + [jnp.zeros((3, features), F32)], axis=0
    )
    result = flat[...].astype(BF)
    for c in range(copies):
        out_ref[c] = result


def expert_kernel(
    dp_ref, x_ref, g0, g1, g2, g3, d0, d1, d2, d3, out_ref, x_in, tails, held, gate, up, hidden, column, y_out, sems, more
):
    dp = dp_ref[0]
    parts, total, features = x_ref.shape
    rows = total - 16
    half = rows // 2
    arriving = {("tails",): pltpu.make_async_copy(x_ref.at[:, pl.ds(rows, 16), :], tails, more.at[8])}
    for p in range(4):
        for i in range(2):
            source = x_ref.at[2 * (dp ^ p) + i, pl.ds(0, rows), :]
            arriving["x", p, i] = pltpu.make_async_copy(source, x_in.at[2 * p + i], more.at[2 * p + i])
        for m in range(3):
            source = (d0, d1, d2, d3)[p] if m == 2 else (g0, g1, g2, g3)[p].at[m]
            arriving[p, m] = pltpu.make_async_copy(source, held.at[p, m], sems.at[p, m])

    def begin(*keys):
        for key in keys:
            arriving[key].start()

    def piece(p):
        return ("x", p, 0), ("x", p, 1), (p, 0), (p, 1)

    begin(("tails",), *piece(0))
    arriving["tails",].wait()
    begin(*piece(1))
    means, squares = [], []
    for q in range(parts):
        tail = tails[q].astype(F32)
        means.append([tail[5 * h : 5 * h + 1] + tail[5 * h + 1 : 5 * h + 2] + tail[5 * h + 2 : 5 * h + 3] for h in (0, 1)])
        squares.append([tail[5 * h + 3 : 5 * h + 4] + tail[5 * h + 4 : 5 * h + 5] for h in (0, 1)])
    for h in (0, 1):
        average = sum(m[h] for m in means) / parts
        shifts = [m[h] - average for m in means]
        spread = (sum(s[h] for s in squares) + features * sum(s * s for s in shifts)) / (parts * features)
        block = jnp.concatenate(shifts + [lax.rsqrt(spread + 1e-5), jnp.zeros((128 - parts - 1, features), F32)], axis=0)
        column[h * half : (h + 1) * half, :] = block.T[0:half]

    def normed(p, i):
        q = 2 * (dp ^ p) + i
        tail = tails[q].astype(F32)
        gain = tail[10:11] + tail[11:12] + tail[12:13]
        at = lax.broadcasted_iota(jnp.int32, (rows, 128), 1)
        shift = jnp.sum(jnp.where(at == q, column[...], 0.0), axis=1, keepdims=True)
        scale = column[:, parts : parts + 1]
        arriving["x", p, i].wait()
        return ((x_in[2 * p + i].astype(F32) + shift) * scale * gain).astype(BF)

    for now in ((0,), (1, 2, 3)):
        x = [jnp.concatenate([normed(p, 0), normed(p, 1)], axis=1) for p in now]
        for p in now:
            arriving[p, 0].wait()
            arriving[p, 1].wait()
        if now[0] == 0:
            begin(*piece(2), *piece(3))
        else:
            begin((0, 2), (1, 2), (2, 2), (3, 2))
        g = sum(dot(part, held[p, 0], NT) for p, part in zip(now, x))
        u = sum(dot(part, held[p, 1], NT) for p, part in zip(now, x))
        if now[0] == 0:
            gate[...] = g
            up[...] = u
        else:
            g = gate[...] + g
            u = up[...] + u
            hidden[...] = (g / (1.0 + jnp.exp(-g)) * u).astype(BF)
    leaving = []
    for p in range(4):
        arriving[p, 2].wait()
    for now in ((0, 1), (2, 3)):
        for p in now:
            y = dot(hidden[...], held[p, 2]).astype(BF)
            for i in range(2):
                y_out[2 * p + i] = y[:, i * features : (i + 1) * features]
        for p in now:
            for i in range(2):
                target = out_ref.at[2 * (dp ^ p) + i]
                leaving.append(pltpu.make_async_copy(y_out.at[2 * p + i], target, more.at[9 + 2 * p + i]))
                leaving[-1].start()
    for copy in leaving:
        copy.wait()


def total_kernel(in_ref, out_ref, flat):
    parts, _, features = in_ref.shape
    blocks, rows, lanes = out_ref.shape
    total = in_ref[0].astype(F32)
    for p in range(1, parts):
        total = total + in_ref[p].astype(F32)
    flat[0 : total.shape[0], :] = total
    groups = features // lanes
    for b in range(blocks):
        block = flat[b * CAP : (b + 1) * CAP, :]
        runs = [block[:, g * lanes : (g + 1) * lanes] for g in range(groups)]
        runs.append(jnp.zeros((rows - groups * CAP, lanes), F32))
        out_ref[b] = jnp.concatenate(runs, axis=0).astype(BF)


def weigh_kernel(term, ids_ref, weight_ref, out_ref):
    wide, places = out_ref.shape
    tokens = ids_ref.shape[1]
    groups = wide // tokens
    experts = EXPERTS
    block = places // experts
    rank = named_and_rank(ids_ref, experts)
    expert = lax.broadcasted_iota(jnp.int32, (experts, tokens), 0)
    weight = jnp.zeros((experts, tokens), F32)
    for k in range(ids_ref.shape[0]):
        weight = weight + jnp.where(ids_ref[k : k + 1, :] == expert, weight_ref[k : k + 1, :], 0.0)
    weight = terms(weight, 2)[term]
    place = lax.broadcasted_iota(jnp.int32, (experts, places), 1)
    start = lax.broadcasted_iota(jnp.int32, (experts, places), 0) * block
    own = jnp.where((place >= start) & (place < start + block), 1.0, 0.0).astype(BF)
    rank = dot(rank.astype(BF), own, TN)
    weight = dot(weight.astype(BF), own, TN)
    at = lax.rem(lax.broadcasted_iota(jnp.int32, (tokens, places), 1), block).astype(F32)
    for g in range(groups):
        out_ref[g * tokens : (g + 1) * tokens, :] = jnp.where(at == rank + g * CAP, weight, 0.0).astype(BF)


def combine_kernel(post_ref, upper_ref, lower_ref, back_ref, out_ref):
    tokens, features = post_ref.shape
    groups = features // back_ref.shape[1]
    back = back_ref[...]
    moe = dot(upper_ref[...], back) + dot(lower_ref[...], back)
    moe = jnp.concatenate([moe[g * tokens : (g + 1) * tokens] for g in range(groups)], axis=1)
    out_ref[...] = (post_ref[...] + moe).astype(BF)


def all_to_all(x, axis):
    return lax.all_to_all(x, axis, split_axis=0, concat_axis=0, tiled=True)


def on_device(
    queries,
    key_heads,
    value_heads,
    doc_ids,
    residual,
    ln_gain,
    expert_ids,
    expert_weight,
    w_gate,
    w_up,
    w_down,
):
    rows = queries.shape[1]
    features = residual.shape[2]
    ctx_count = lax.axis_size("ctx")
    tp_count = lax.axis_size("tp")
    dp_index = lax.axis_index("dp").reshape(1)
    ctx_index = lax.axis_index("ctx").reshape(1)
    ids = expert_ids[0].T
    weight = expert_weight[0].T
    hidden_units = w_down.shape[1]

    other_chip = [(i, i ^ 2) for i in range(4)]
    other_core = [(i, i ^ 1) for i in range(4)]
    down = w_down[0]
    v_first = rows - 16
    both, rest = call(
        stack_kernel,
        (
            jax.ShapeDtypeStruct((2,) + down.shape, BF),
            jax.ShapeDtypeStruct((ctx_count, rows - v_first, HEAD_DIM), BF),
        ),
        [ANY] * 3,
        [
            pltpu.VMEM((2,) + down.shape, BF),
            pltpu.VMEM((rows - v_first, HEAD_DIM), BF),
            pltpu.SemaphoreType.DMA((3,)),
            pltpu.SemaphoreType.DMA((2 + ctx_count,)),
        ],
        out_spec=ANY,
        limit=FULL,
        name="stack",
    )(w_gate[0].T, w_up[0].T, value_heads[0])
    both_chip = lax.ppermute(both, "dp", other_chip)

    docs_row = jnp.broadcast_to(doc_ids.astype(BF), (8, rows))
    packed = jnp.concatenate([key_heads[0], value_heads[0, :v_first], docs_row], axis=0)
    rest = all_to_all(rest, "ctx")
    kv = lax.all_gather(packed, "ctx", axis=0)
    back = -(-(REACH - 1) // rows)
    group = queries.shape[2] // HEAD_DIM
    block = -(-(features // 128 * CAP + 5) // 8) * 8
    post, outgoing = call(
        functools.partial(attend_kernel, back, v_first),
        (jax.ShapeDtypeStruct((rows, features), F32), jax.ShapeDtypeStruct((ctx_count, block, 128), BF)),
        [SMEM] + [VMEM] * 6,
        [pltpu.VMEM((back + 1, group * rows, rows), F32)],
        name="attend",
    )(ctx_index, queries[0], kv, rest, doc_ids[0].astype(F32).reshape(rows, 1), residual[0], ids)
    outgoing, down, both, both_chip = lax.optimization_barrier((outgoing, down, both, both_chip))
    landed = all_to_all(outgoing, "ctx")
    down_chip = lax.ppermute(down, "dp", other_chip)
    both_core = lax.ppermute(both, "dp", other_core)
    both_far = lax.ppermute(both_chip, "dp", other_core)
    down_core = lax.ppermute(down, "dp", other_core)
    total_rows = ctx_count * CAP
    copies = call(
        spread_kernel,
        jax.ShapeDtypeStruct((tp_count, total_rows + 16, features), BF),
        [VMEM] * 2,
        [pltpu.VMEM((total_rows + 16, features), F32)],
        name="spread",
    )(landed, ln_gain.reshape(1, features))
    copies, down_chip = lax.optimization_barrier((copies, down_chip))
    arrived = all_to_all(copies, "tp")
    down_far = lax.ppermute(down_chip, "dp", other_core)
    partial = call(
        expert_kernel,
        jax.ShapeDtypeStruct((tp_count, total_rows, features), BF),
        [SMEM] + [ANY] * 9,
        [
            pltpu.VMEM((tp_count, total_rows, features), BF),
            pltpu.VMEM((tp_count, 16, features), BF),
            pltpu.VMEM((4, 3) + down.shape, BF),
            pltpu.VMEM((total_rows, hidden_units), F32),
            pltpu.VMEM((total_rows, hidden_units), F32),
            pltpu.VMEM((total_rows, hidden_units), BF),
            pltpu.VMEM((total_rows, 128), F32),
            pltpu.VMEM((tp_count, total_rows, features), BF),
            pltpu.SemaphoreType.DMA((4, 3)),
            pltpu.SemaphoreType.DMA((17,)),
        ],
        out_spec=ANY,
        limit=FULL,
        flops=6 * total_rows * hidden_units * features * tp_count,
        moved=24 << 20,
        name="expert",
    )(dp_index, arrived, both, both_core, both_chip, both_far, down, down_core, down_chip, down_far)
    block = -(-(features // 128 * CAP) // 8) * 8

    def weigh(term, ids):
        return call(
            functools.partial(weigh_kernel, term),
            jax.ShapeDtypeStruct((features, ctx_count * block), BF),
            [VMEM] * 2,
            name="weigh",
        )(ids, weight)

    partial, ids_later = lax.optimization_barrier((partial, ids))
    groups = all_to_all(partial, "tp")
    upper, lower = weigh(0, ids_later), weigh(1, ids_later)
    groups, upper, lower = lax.optimization_barrier((groups, upper, lower))
    expert_out = call(
        total_kernel,
        jax.ShapeDtypeStruct((ctx_count, block, 128), BF),
        [VMEM],
        [pltpu.VMEM((total_rows + 16, features), F32)],
        name="total",
    )(groups)
    returned = all_to_all(expert_out, "ctx")
    mixed = call(
        combine_kernel,
        jax.ShapeDtypeStruct((rows, features), BF),
        [VMEM] * 4,
        name="combine",
    )(post, upper, lower, returned.reshape(ctx_count * block, 128))
    return mixed[None]


def solution(mesh):
    placed = (
        P("dp", "ctx", "tp"),
        P("dp", "ctx", "tp"),
        P("dp", "ctx", "tp"),
        P("dp", "ctx"),
        P("dp", "ctx", "tp"),
        P("tp"),
        P("dp", "ctx", None),
        P("dp", "ctx", None),
        P("ctx", "dp", "tp"),
        P("ctx", "dp", "tp"),
        P("ctx", "tp", "dp"),
    )
    return jax.shard_map(
        on_device, mesh=mesh, in_specs=placed, out_specs=P("dp", "ctx", "tp"), check_vma=False
    )
```
